512 devices in a mesh: gz: 32 (over z_hi, y), ch: 16 (over x, z_lo, core).
Axes of the slice: x: 4, y: 8, z: 8 (z_hi: 4, z_lo: 2; z = z_hi * 2 + z_lo), core: 2. Of those that a mesh axis runs over, the one named last changes fastest.
Arguments:
- coarse: bfloat16 [256, 32, 128], P('ch', 'gz'), may hold values from -102 to 102
- encoder_skip: bfloat16 [128, 64, 512], P('ch', 'gz'), may hold values from -102 to 102
- up_weight: bfloat16 [27, 128, 256], P(None, None, 'ch'), may hold values from -0.21875 to 0.21875
- first_up: bfloat16 [27, 128, 128], P(None, None, 'ch'), may hold values from -0.078125 to 0.078125
- first_skip: bfloat16 [27, 128, 128], P(None, None, 'ch'), may hold values from -0.078125 to 0.078125
- second_weight: bfloat16 [27, 128, 128], P(None, None, 'ch'), may hold values from -0.109375 to 0.109375
- cotangent: bfloat16 [128, 64, 512], P('ch', 'gz'), may hold values from -33 to 33
Outputs:
- decoded: bfloat16 [128, 64, 512], P('ch', 'gz')
- grad_coarse: bfloat16 [256, 32, 128], P('ch', 'gz')
- grad_skip: bfloat16 [128, 64, 512], P('ch', 'gz')
- grad_up_weight: float32 [27, 128, 256], P(None, None, 'ch')
- grad_first_up: float32 [27, 128, 128], P(None, None, 'ch')
- grad_first_skip: float32 [27, 128, 128], P(None, None, 'ch')
- grad_second: float32 [27, 128, 128], P(None, None, 'ch')
The draws below stay inside these ranges and needn't reach their ends.
All inputs are finite; a program needn't handle non-finite values.
Results may differ from the reference program's by a relative error of at most 0.015.
Values may be sent and summed in bfloat16 or wider, within the bound.
No kernel may reach another device: no remote copies, remote signals or barrier semaphores. Data moves between devices by JAX's collectives and lax.ppermute only.
A program may use at most 64 MiB of HBM per device.

```python
import math
import jax
import jax.numpy as jnp
from jax import lax

C_IN = 256
C_OUT = 128
YC = 8
XC = 16
ZC = 32
NZ = 64
SLAB_CELLS = 1024


def rising_field(key, full_shape, ceiling, rough_part):
    channels, planes, plane_cells = full_shape
    height = jnp.arange(planes, dtype=jnp.float32) / (planes - 1)
    growth = jnp.exp(jnp.log(ceiling) * height)[None, :, None]
    key_scale, key_offset = jax.random.split(key, 2)
    channel_scale = jnp.exp(jnp.log(2.0) * jax.random.uniform(key_scale, (channels, 1, 1)))
    offset = 0.5 * jnp.clip(jax.random.normal(key_offset, (channels, 1, 1)), -2.0, 2.0) * (1.0 + 2.0 * height)[None, :, None]
    return channel_scale * growth * rough_part + offset


def draw_coarse(key, part):
    key = jax.random.fold_in(key, 11)
    key_rough, key_rest = jax.random.split(key)
    full_shape = (C_IN, ZC, YC * XC)
    rough_part = jnp.clip(jax.random.normal(key_rough, full_shape), -4.0, 4.0)
    result = rising_field(key_rest, full_shape, 10.0, rough_part)
    return result.astype(jnp.bfloat16)


def draw_encoder_skip(key, part):
    key = jax.random.fold_in(key, 23)
    key_rough, key_rest = jax.random.split(key)
    full_shape = (C_OUT, NZ, 4 * YC * XC)
    rough_part = jnp.clip(jax.random.normal(key_rough, full_shape), -4.0, 4.0)
    result = rising_field(key_rest, full_shape, 10.0, rough_part)
    return result.astype(jnp.bfloat16)


def draw_cotangent(key, part):
    key = jax.random.fold_in(key, 37)
    key_rough, key_rest = jax.random.split(key)
    full_shape = (C_OUT, NZ, 4 * YC * XC)
    rough_part = jnp.clip(jax.random.normal(key_rough, full_shape), -4.0, 4.0)
    result = rising_field(key_rest, full_shape, 3.0, rough_part)
    return result.astype(jnp.bfloat16)


def block_levels(rng, shape, pieces, smallest, top_value):
    level, own = 1.0, jax.random.fold_in(rng, 6)
    for position, blocks in pieces:
        steps = jnp.exp(jax.random.uniform(jax.random.fold_in(own, position), (blocks,), jnp.float32, smallest / len(pieces), top_value / len(pieces)))
        level = level * jnp.repeat(steps, shape[position] // blocks).reshape([-1 if axis == position else 1 for axis in range(len(shape))])
    return level


def gaussian(rng, dims, scale, bound, cuts=(), kind=jnp.bfloat16):
    values = scale * jax.random.normal(rng, dims, jnp.float32)
    if cuts:
        values = values * block_levels(rng, dims, cuts, -0.22, 0.18)
    return jnp.clip(values, -bound, bound).astype(kind)


def setup_inputs(seed: int = 0) -> dict:
    key_list = jax.random.split(jax.random.key(seed), 8)
    return {
        "coarse": draw_coarse(jax.random.fold_in(key_list[7], 71), 0),
        "encoder_skip": draw_encoder_skip(jax.random.fold_in(key_list[7], 71), 0),
        "up_weight": gaussian(key_list[2], (27, C_OUT, C_IN), (27 * C_IN // 8) ** -0.5, 0.21875, ((2, 16),)),
        "first_up": gaussian(key_list[3], (27, C_OUT, C_OUT), (54 * C_OUT) ** -0.5, 0.078125, ((2, 16),)),
        "first_skip": gaussian(key_list[4], (27, C_OUT, C_OUT), (54 * C_OUT) ** -0.5, 0.078125, ((2, 16),)),
        "second_weight": gaussian(key_list[5], (27, C_OUT, C_OUT), (27 * C_OUT) ** -0.5, 0.109375, ((2, 16),)),
        "cotangent": draw_cotangent(jax.random.fold_in(key_list[7], 71), 0),
    }


LEAK_SLOPE = 0.01
KINK_WIDTH = 0.01
NORM_EPS = 1e-05
PARITY_TAPS = (((1, 0),), ((2, 0), (0, 1)))

def plane_shift(values, step_y, step_x, columns):
    extent = values.shape[-1]
    margins = [(0, 0)] * (values.ndim - 1) + [(columns + 1, columns + 1)]
    padded = jnp.pad(values, margins)
    offset_at = columns + 1 + step_y * columns + step_x
    shifted = lax.slice_in_dim(padded, offset_at, offset_at + extent, axis=values.ndim - 1)
    column = jnp.arange(extent, dtype=jnp.int32) % columns + step_x
    inside = (column >= 0) & (column < columns)
    return jnp.where(inside, shifted, jnp.zeros_like(shifted))

def activate(inputs):
    smooth = jnp.sqrt(inputs * inputs + KINK_WIDTH)
    return 0.5 * (1.0 + LEAK_SLOPE) * inputs + 0.5 * (1.0 - LEAK_SLOPE) * smooth

def activate_slope(inputs):
    return 0.5 * (1.0 + LEAK_SLOPE) + 0.5 * (1.0 - LEAK_SLOPE) * inputs / jnp.sqrt(inputs * inputs + KINK_WIDTH)

def up_forward(extended, weights, columns):
    channels = extended.shape[0]
    planes = extended.shape[1] - 1
    plane_cells = extended.shape[2]
    shifted = {}
    for y_off in (0, 1):
        for x_off in (0, 1):
            shifted[y_off, x_off] = plane_shift(extended, y_off, x_off, columns)
    results = []
    for z_par in (0, 1):
        for y_par in (0, 1):
            for x_par in (0, 1):
                left_parts = []
                right_parts = []
                for k_z, z_off in PARITY_TAPS[z_par]:
                    for k_y, y_off in PARITY_TAPS[y_par]:
                        for k_x, x_off in PARITY_TAPS[x_par]:
                            left_parts.append(weights[k_z * 9 + k_y * 3 + k_x])
                            source = shifted[y_off, x_off][:, z_off:z_off + planes]
                            right_parts.append(source.reshape(channels, planes * plane_cells))
                matrix = jnp.concatenate(left_parts, axis=1)
                stacked = jnp.concatenate(right_parts, axis=0)
                results.append(jnp.dot(matrix, stacked, preferred_element_type=jnp.float32))
    return jnp.stack(results)

def alternate(parities, planes, columns):
    outputs = parities.shape[1]
    coarse_rows = parities.shape[2] // (planes * columns)
    arranged = parities.reshape(2, 2, 2, outputs, planes, coarse_rows, columns)
    arranged = jnp.transpose(arranged, (3, 4, 0, 5, 1, 6, 2))
    return arranged.reshape(outputs, 2 * planes, 4 * coarse_rows * columns)

def split_parity(fine_grad, columns):
    outputs, planes = (fine_grad.shape[0], fine_grad.shape[1])
    coarse_rows = fine_grad.shape[2] // (4 * columns)
    arranged = fine_grad.reshape(outputs, planes, coarse_rows, 2, columns, 2)
    arranged = jnp.transpose(arranged, (3, 5, 0, 1, 2, 4))
    return arranged.reshape(2, 2, outputs, planes, coarse_rows * columns)

def up_backward(grad_ext, coarse, weights, columns):
    outputs = grad_ext.shape[0]
    channels, planes = (coarse.shape[0], coarse.shape[1])
    cells_all = planes * coarse.shape[2]
    flat_coarse = coarse.reshape(channels, cells_all)
    chosen = {(0, 0): grad_ext[:, 1:2 * planes:2], (1, 0): grad_ext[:, 2:2 * planes + 1:2], (1, 1): grad_ext[:, 0:2 * planes:2]}
    parted = {}
    for choice_key in chosen:
        parted[choice_key] = split_parity(chosen[choice_key], columns)
    d_coarse = jnp.zeros((channels, cells_all), jnp.float32)
    tap_grads = [None] * 27
    for z_par in (0, 1):
        for y_par in (0, 1):
            for x_par in (0, 1):
                left_parts = []
                right_parts = []
                for k_z, z_off in PARITY_TAPS[z_par]:
                    for k_y, y_off in PARITY_TAPS[y_par]:
                        for k_x, x_off in PARITY_TAPS[x_par]:
                            tap_index = k_z * 9 + k_y * 3 + k_x
                            source = parted[z_par, z_off][y_par, x_par]
                            shifted_grad = plane_shift(source, -y_off, -x_off, columns).reshape(outputs, cells_all)
                            left_parts.append(weights[tap_index])
                            right_parts.append(shifted_grad)
                            tap_grads[tap_index] = jnp.dot(shifted_grad, flat_coarse.T, preferred_element_type=jnp.float32)
                matrix = jnp.concatenate(left_parts, axis=0)
                stacked = jnp.concatenate(right_parts, axis=0)
                d_coarse = d_coarse + jnp.dot(matrix.T, stacked, preferred_element_type=jnp.float32)
    return (d_coarse.reshape(coarse.shape), jnp.stack(tap_grads))

def conv_forward(padded, weights, columns):
    channels, planes, plane_cells = (padded.shape[0], padded.shape[1] - 2, padded.shape[2])
    result = jnp.zeros((weights.shape[1], planes * plane_cells), jnp.float32)
    for tap_index in range(27):
        k_z, k_y, k_x = (tap_index // 9, tap_index // 3 % 3, tap_index % 3)
        source = plane_shift(padded[:, k_z:k_z + planes], k_y - 1, k_x - 1, columns)
        result = result + jnp.dot(weights[tap_index], source.reshape(channels, -1), preferred_element_type=jnp.float32)
    return result.reshape(weights.shape[1], planes, plane_cells)

def conv_backward(grad_padded, padded, weights, columns):
    outputs, planes, plane_cells = (grad_padded.shape[0], grad_padded.shape[1] - 2, grad_padded.shape[2])
    channels = padded.shape[0]
    interior = grad_padded[:, 1:planes + 1].reshape(outputs, -1)
    d_input = jnp.zeros((channels, planes * plane_cells), jnp.float32)
    tap_grads = []
    for tap_index in range(27):
        k_z, k_y, k_x = (tap_index // 9, tap_index // 3 % 3, tap_index % 3)
        source = plane_shift(grad_padded[:, 2 - k_z:2 - k_z + planes], 1 - k_y, 1 - k_x, columns)
        d_input = d_input + jnp.dot(weights[tap_index].T, source.reshape(outputs, -1), preferred_element_type=jnp.float32)
        shifted = plane_shift(padded[:, k_z:k_z + planes], k_y - 1, k_x - 1, columns)
        tap_grads.append(jnp.dot(interior, shifted.reshape(channels, -1).T, preferred_element_type=jnp.float32))
    return (d_input.reshape(channels, planes, plane_cells), jnp.stack(tap_grads))

def normalize(summed):
    centre = lax.optimization_barrier(jnp.mean(summed, axis=(1, 2), keepdims=True))
    spread = lax.optimization_barrier(jnp.mean(jnp.square(summed - centre), axis=(1, 2), keepdims=True))
    inverse = lax.rsqrt(spread + NORM_EPS)
    return ((summed - centre) * inverse, inverse)

def norm_back(slope_grad, normed, inverse):
    mean_grad = lax.optimization_barrier(jnp.mean(slope_grad, axis=(1, 2), keepdims=True))
    mean_cross = lax.optimization_barrier(jnp.mean(slope_grad * normed, axis=(1, 2), keepdims=True))
    return inverse * (slope_grad - mean_grad - normed * mean_cross)

def z_pad(values):
    return jnp.pad(values, ((0, 0), (1, 1), (0, 0)))

def reference(coarse, encoder_skip, up_weight, first_up, first_skip, second_weight, cotangent):
    fine_columns = 2 * XC
    extended = jnp.concatenate([coarse, jnp.zeros_like(coarse[:, :1])], axis=1)
    upsampled = alternate(up_forward(extended, up_weight, XC), coarse.shape[1], XC).astype(jnp.bfloat16)
    first_in = z_pad(jnp.concatenate([upsampled, encoder_skip], axis=0))
    first_weight = jnp.concatenate([first_up, first_skip], axis=2)
    first_normed, first_inverse = normalize(conv_forward(first_in, first_weight, fine_columns))
    hidden = activate(first_normed).astype(jnp.bfloat16)
    second_in = z_pad(hidden)
    second_normed, second_inverse = normalize(conv_forward(second_in, second_weight, fine_columns))
    decoded = activate(second_normed).astype(jnp.bfloat16)
    slope_two = cotangent.astype(jnp.float32) * activate_slope(second_normed)
    d_second = norm_back(slope_two, second_normed, second_inverse).astype(jnp.bfloat16)
    d_hidden, grad_second = conv_backward(z_pad(d_second), second_in, second_weight, fine_columns)
    slope_one = d_hidden * activate_slope(first_normed)
    d_first = norm_back(slope_one, first_normed, first_inverse).astype(jnp.bfloat16)
    d_joined, grad_first = conv_backward(z_pad(d_first), first_in, first_weight, fine_columns)
    d_up = d_joined[:C_OUT].astype(jnp.bfloat16)
    grad_skip = d_joined[C_OUT:].astype(jnp.bfloat16)
    grad_ext = jnp.concatenate([jnp.zeros_like(d_up[:, :1]), d_up], axis=1)
    d_coarse, grad_up = up_backward(grad_ext, coarse, up_weight, XC)
    factor = 1.0 / math.sqrt(SLAB_CELLS)
    return (decoded, d_coarse.astype(jnp.bfloat16), grad_skip, grad_up * factor, grad_first[:, :, :C_OUT] * factor, grad_first[:, :, C_OUT:] * factor, grad_second * factor)
```

```python
import math

import jax
import jax.numpy as jnp
from jax import lax
from jax.experimental import pallas as pl
from jax.experimental.pallas import tpu as pltpu
from jax.sharding import PartitionSpec as P

C_OUT = 128
XC = 16
YC = 8
COARSE = YC * XC
FINE = 4 * COARSE
SLAB = 2 * FINE
HALOED = 4 * FINE
LEAK_SLOPE = 0.01
KINK_WIDTH = 0.01
NORM_EPS = 1e-05
PARITY = (((1, 0),), ((2, 0), (0, 1)))
GRAD_ROWS = 1280

f32 = jnp.float32
bf16 = jnp.bfloat16


def activate(u):
    q = u * u + KINK_WIDTH
    return 0.5 * (1.0 + LEAK_SLOPE) * u + 0.5 * (1.0 - LEAK_SLOPE) * (q * lax.rsqrt(q))


def activate_slope(u):
    return 0.5 * (1.0 + LEAK_SLOPE) + 0.5 * (1.0 - LEAK_SLOPE) * (
        u * lax.rsqrt(u * u + KINK_WIDTH)
    )


def shift(values, step_y, step_x, rows, columns):
    if step_y == 0 and step_x == 0:
        return values
    extent = values.shape[-1]
    cell = lax.broadcasted_iota(jnp.int32, (1, extent), 1)
    column = cell % columns + step_x
    row = cell // columns % rows + step_y
    inside = (column >= 0) & (column < columns) & (row >= 0) & (row < rows)
    moved = pltpu.roll(values, (-(step_y * columns + step_x)) % extent, 1)
    return moved * jnp.where(inside, 1.0, 0.0)


def fine_shift(values, step_y, step_x):
    return shift(values, step_y, step_x, 2 * YC, 2 * XC)


def coarse_shift(values, step_y, step_x):
    return shift(values, step_y, step_x, YC, XC)


def interleave_matrix(transposed):
    fine_dim = 0 if transposed else 1
    cell = lax.broadcasted_iota(jnp.int32, (FINE, FINE), fine_dim)
    other = lax.broadcasted_iota(jnp.int32, (FINE, FINE), 1 - fine_dim)
    y, x = cell // (2 * XC), cell % (2 * XC)
    source = ((y % 2) * 2 + x % 2) * COARSE + (y // 2) * XC + x // 2
    return jnp.where(source == other, 1.0, 0.0).astype(bf16)


def edge_mask(slab, slabs):
    plane = lax.broadcasted_iota(jnp.int32, (1, HALOED), 1) // FINE
    outside = ((plane == 0) & (slab == 0)) | ((plane == 3) & (slab == slabs - 1))
    return jnp.where(outside, 0.0, 1.0)


def as_row(column):
    return jnp.transpose(jnp.broadcast_to(column, (C_OUT, C_OUT)))[:1]


def as_column(row):
    return jnp.transpose(jnp.broadcast_to(row, (C_OUT, C_OUT)))[:, :1]


def call(kernel, outs, args, scratch=(), megabytes=24):
    specs = [pl.BlockSpec(memory_space=pltpu.SMEM)]
    specs += [pl.BlockSpec(memory_space=pltpu.VMEM)] * (len(args) - 1)
    return pl.pallas_call(
        kernel,
        out_shape=[jax.ShapeDtypeStruct(shape, dtype) for shape, dtype in outs],
        in_specs=specs,
        out_specs=[pl.BlockSpec(memory_space=pltpu.VMEM)] * len(outs),
        scratch_shapes=list(scratch),
        compiler_params=pltpu.CompilerParams(vmem_limit_bytes=megabytes * 2**20),
    )(*args)


def up_kernel(place, mixed, own_skip, skip_low, skip_high, first_up, first_skip, partial, joined, unfolded):
    slab = place[0]
    packed = mixed[...]
    weights = packed[:, :, :256].reshape(256, 256)
    mixture = []
    for plane in range(3):
        source = packed[:, :, 256 + plane * COARSE : 256 + (plane + 1) * COARSE].reshape(256, COARSE)
        mixture.append(
            lax.dot_general(weights, source, (((0,), (0,)), ((), ())), preferred_element_type=f32)
        )
    rows = []
    for sources in (((2, 0), (0, 1)), ((1, 1),), ((2, 1), (0, 2)), ((1, 2),)):
        cells = []
        for y_par in (0, 1):
            for x_par in (0, 1):
                total = None
                for k_z, plane in sources:
                    for k_y, y_off in PARITY[y_par]:
                        for k_x, x_off in PARITY[x_par]:
                            tap = k_z * 9 + k_y * 3 + k_x
                            term = coarse_shift(mixture[plane][tap * 8 : tap * 8 + 8], y_off, x_off)
                            total = term if total is None else total + term
                cells.append(total)
        rows.append(jnp.concatenate(cells, axis=1))
    spread = jnp.concatenate(rows, axis=0).astype(bf16)
    fine = jnp.dot(spread, interleave_matrix(False), preferred_element_type=f32)
    first_inside = jnp.where(slab == 0, 0.0, 1.0)
    upsampled = jnp.concatenate(
        [fine[0:8] * first_inside, fine[8:16], fine[16:24], fine[24:32]], axis=1
    )
    skip = jnp.concatenate(
        [skip_low[...].astype(f32), own_skip[...].astype(f32), skip_high[...].astype(f32)], axis=1
    )
    features = jnp.concatenate([upsampled, skip], axis=0)
    joined[...] = features.astype(bf16)
    for tap in range(9):
        unfolded[tap * 16 : tap * 16 + 16, :] = fine_shift(features, tap // 3 - 1, tap % 3 - 1).astype(bf16)
    total = jnp.zeros((C_OUT, SLAB), f32)
    for k_z in range(3):
        matrix = []
        for tap in range(9):
            up_part = first_up[k_z * 9 + tap].astype(f32)
            skip_part = first_skip[k_z * 9 + tap].astype(f32)
            matrix.append(jnp.concatenate([up_part, skip_part], axis=0))
        matrix = jnp.concatenate(matrix, axis=0).astype(bf16)
        total = total + lax.dot_general(
            matrix,
            unfolded[:, k_z * FINE : k_z * FINE + SLAB],
            (((0,), (0,)), ((), ())),
            preferred_element_type=f32,
        )
    partial[...] = total.reshape(16, 8, SLAB)


def first_sum_kernel(place, parts, pre, low, high, stats):
    total = jnp.sum(parts[...], axis=0)
    pre[...] = total
    low[...] = total[:, :FINE]
    high[...] = total[:, FINE:]
    mean = jnp.sum(total, axis=1, keepdims=True) / SLAB
    deviation = total - mean
    square = jnp.sum(deviation * deviation, axis=1, keepdims=True)
    lane = lax.broadcasted_iota(jnp.int32, (8, 128), 1)
    tile = jnp.where(lane < 64, mean, square)
    stats[...] = jnp.broadcast_to(tile[None], stats.shape)


def first_norm_kernel(place, pre, low, high, stats, cotangent, cot_low, cot_high, packed):
    slabs = stats.shape[0]
    gathered = stats[...]
    means = gathered[:, :, :1]
    mean = jnp.sum(means, axis=0) / slabs
    apart = means - mean[None]
    square = jnp.sum(gathered[:, :, 127:] + SLAB * apart * apart, axis=0)
    inverse = lax.rsqrt(square / (slabs * SLAB) + NORM_EPS)
    lower = jnp.concatenate([low[...], pre[:, :FINE]], axis=1)
    upper = jnp.concatenate([pre[:, FINE:], high[...]], axis=1)
    cot = cotangent[...].astype(f32)
    cot_lower = jnp.concatenate([cot_low[...].astype(f32), cot[:, :FINE]], axis=1)
    cot_upper = jnp.concatenate([cot[:, FINE:], cot_high[...].astype(f32)], axis=1)
    wide = jnp.broadcast_to(inverse, (8, 128))
    main = wide.astype(bf16).astype(f32)
    block = jnp.concatenate(
        [
            jnp.concatenate([(lower - mean) * inverse, cot_lower, main], axis=1),
            jnp.concatenate([(upper - mean) * inverse, cot_upper, wide - main], axis=1),
        ],
        axis=0,
    ).astype(bf16)
    for target in range(16):
        packed[target] = block


def read_planes(packed, block, offset):
    pair = packed[pl.ds(2 * block, 2), :, offset : offset + SLAB].astype(f32)
    return jnp.concatenate([pair[:, :8].reshape(16, SLAB), pair[:, 8:].reshape(16, SLAB)], axis=1)


def unfold_block(values, unfolded, block, sign):
    for tap in range(9):
        moved = fine_shift(values, sign * (tap // 3 - 1), sign * (tap % 3 - 1))
        unfolded[pl.ds(pl.multiple_of(tap * 128 + block * 16, 16), 16), :] = moved.astype(bf16)


def tap_matrix(weights, tap, first):
    both = weights[:, tap].astype(f32)
    return both[:, first * 8 : first * 8 + 8].reshape(C_OUT, C_OUT)


def second_conv_kernel(place, packed, weights, pre, low, high, stats, unfolded, matrix):
    mask = edge_mask(place[0], stats.shape[0])

    def prepare(block, carry):
        hidden = activate(read_planes(packed, block, 0)).astype(bf16).astype(f32) * mask
        unfold_block(hidden, unfolded, block, 1)
        return carry

    lax.fori_loop(0, 8, prepare, 0)
    for tap in range(27):
        matrix[:, tap * 128 : tap * 128 + 128] = jnp.transpose(tap_matrix(weights, tap, 0)).astype(bf16)
    total = jnp.zeros((C_OUT, SLAB), f32)
    for k_z in range(3):
        total = total + jnp.dot(
            matrix[:, k_z * 1152 : k_z * 1152 + 1152],
            unfolded[:, k_z * FINE : k_z * FINE + SLAB],
            preferred_element_type=f32,
        )
    pre[...] = total
    mean = jnp.sum(total, axis=1, keepdims=True) / SLAB
    deviation = total - mean
    square = jnp.sum(deviation * deviation, axis=1, keepdims=True)
    low[...] = deviation[:, :FINE].astype(bf16)
    high[...] = deviation[:, FINE:].astype(bf16)
    row = lax.broadcasted_iota(jnp.int32, (8, 128), 0)
    tile = jnp.where(row < 4, as_row(mean), as_row(square))
    stats[...] = jnp.broadcast_to(tile[None], stats.shape)


def second_norm_kernel(
    place, pre, low, high, stats, packed, decoded, normed, slope, inverse_out, sums
):
    slab, share = place[0], place[1]
    slabs = stats.shape[0]
    gathered = stats[...]
    means = gathered[:, 0:1]
    mean_row = jnp.sum(means, axis=0) / slabs
    apart = means - mean_row[None]
    square = jnp.sum(gathered[:, 7:8] + SLAB * apart * apart, axis=0)
    inverse_row = lax.rsqrt(square / (slabs * SLAB) + NORM_EPS)
    inverse_out[...] = jnp.broadcast_to(inverse_row, inverse_out.shape)
    below = stats[jnp.maximum(slab - 1, 0)][0:1] - mean_row
    above = stats[jnp.minimum(slab + 1, slabs - 1)][0:1] - mean_row
    mean, inverse = as_column(mean_row), as_column(inverse_row)
    normed[:, :FINE] = (low[...].astype(f32) + as_column(below)) * inverse
    normed[:, FINE : 3 * FINE] = (pre[...] - mean) * inverse
    normed[:, 3 * FINE :] = (high[...].astype(f32) + as_column(above)) * inverse
    own = normed[pl.ds(pl.multiple_of(share * 8, 8), 8), FINE : 3 * FINE]
    decoded[...] = activate(own).astype(bf16)

    def prepare(block, carry):
        at = pl.ds(pl.multiple_of(block * 16, 16), 16)
        slope[at, :] = read_planes(packed, block, SLAB) * activate_slope(normed[at, :])
        return carry

    lax.fori_loop(0, 8, prepare, 0)
    inner = slope[:, FINE : 3 * FINE]
    one = as_row(jnp.sum(inner, axis=1, keepdims=True))
    two = as_row(jnp.sum(inner * normed[:, FINE : 3 * FINE], axis=1, keepdims=True))
    row = lax.broadcasted_iota(jnp.int32, (8, 128), 0)
    sums[...] = jnp.broadcast_to(jnp.where(row < 4, one, two)[None], sums.shape)


def total_means(sums):
    totals = jnp.sum(sums[...], axis=0) / (sums.shape[0] * SLAB)
    return as_column(totals[0:1]), as_column(totals[7:8])


def second_back_kernel(
    place, normed, slope, inverse_row, sums_in, packed, weights,
    low, high, slope_one, sums, weight_grad, unfolded, matrix, grads, columns, own_cols,
):
    slab, share = place[0], place[1]
    mask = edge_mask(slab, sums.shape[0])
    mean_grad, mean_cross = total_means(sums_in)
    columns[0] = jnp.broadcast_to(mean_grad, (C_OUT, 128))
    columns[1] = jnp.broadcast_to(mean_cross, (C_OUT, 128))
    columns[2] = jnp.broadcast_to(as_column(inverse_row[0:1]), (C_OUT, 128))

    def prepare(block, carry):
        at = pl.ds(pl.multiple_of(block * 16, 16), 16)
        grad = columns[2, at, :1] * (slope[at, :] - columns[0, at, :1] - normed[at, :] * columns[1, at, :1])
        grad = grad.astype(bf16).astype(f32) * mask
        grads[at, :] = grad[:, FINE : 3 * FINE].astype(bf16)
        unfold_block(grad, unfolded, block, -1)
        return carry

    lax.fori_loop(0, 8, prepare, 0)
    for tap in range(27):
        matrix[:, tap * 128 : tap * 128 + 128] = tap_matrix(weights, tap, 0).astype(bf16)
    total = jnp.zeros((C_OUT, SLAB), f32)
    for k_z in range(3):
        total = total + jnp.dot(
            matrix[:, k_z * 1152 : k_z * 1152 + 1152],
            unfolded[:, (2 - k_z) * FINE : (2 - k_z) * FINE + SLAB],
            preferred_element_type=f32,
        )
    low[...] = total[:, :FINE].astype(bf16)
    high[...] = total[:, FINE:].astype(bf16)
    both = packed[:, :, :SLAB].astype(f32)
    first_normed = jnp.concatenate(
        [both[:, :8, FINE:].reshape(C_OUT, FINE), both[:, 8:, :FINE].reshape(C_OUT, FINE)], axis=1
    )
    inner = total * activate_slope(first_normed)
    slope_one[...] = inner
    one = as_row(jnp.sum(inner, axis=1, keepdims=True))
    two = as_row(jnp.sum(inner * first_normed, axis=1, keepdims=True))
    row = lax.broadcasted_iota(jnp.int32, (8, 128), 0)
    sums[...] = jnp.broadcast_to(jnp.where(row < 4, one, two)[None], sums.shape)
    own = packed[share].astype(f32)
    own = jnp.concatenate([own[:8, :SLAB], own[8:, :SLAB]], axis=1)
    own = activate(own).astype(bf16).astype(f32) * mask
    for tap in range(9):
        moved = fine_shift(own, tap // 3 - 1, tap % 3 - 1)
        for k_z in range(3):
            at = (k_z * 9 + tap) * 8
            own_cols[at : at + 8, :] = moved[:, k_z * FINE : k_z * FINE + SLAB]
    weight_grad[...] = lax.dot_general(
        own_cols[...].astype(bf16), grads[...], (((1,), (1,)), ((), ())), preferred_element_type=f32
    )


def first_back_kernel(
    place, slope, low, high, sums_in, packed, weights, first_skip, up_weight, coarse, joined, second_grad,
    skip_grad, coarse_own, coarse_next, weight_grads,
    unfolded, matrix, grads, columns, own_cols, spread, up_matrix,
):
    slab = place[0]
    mask = edge_mask(slab, sums_in.shape[0])
    mean_grad, mean_cross = total_means(sums_in)
    columns[0] = jnp.broadcast_to(mean_grad, (C_OUT, 128))
    columns[1] = jnp.broadcast_to(mean_cross, (C_OUT, 128))
    wide = packed[:, :, 2 * SLAB :].astype(f32)
    columns[2] = (wide[:, :8] + wide[:, 8:]).reshape(C_OUT, 128)

    def prepare(block, carry):
        at = pl.ds(pl.multiple_of(block * 16, 16), 16)
        normed = read_planes(packed, block, 0)
        bottom = low[at, :].astype(f32) * activate_slope(normed[:, :FINE])
        top = high[at, :].astype(f32) * activate_slope(normed[:, 3 * FINE :])
        inner = jnp.concatenate([bottom, slope[at, :], top], axis=1)
        grad = columns[2, at, :1] * (inner - columns[0, at, :1] - normed * columns[1, at, :1])
        grad = grad.astype(bf16).astype(f32) * mask
        grads[at, :] = grad[:, FINE : 3 * FINE].astype(bf16)
        unfold_block(grad, unfolded, block, -1)
        return carry

    lax.fori_loop(0, 8, prepare, 0)
    for tap in range(27):
        at = slice(tap * 128, tap * 128 + 128)
        skip_part = jnp.concatenate([first_skip[tap].astype(f32), jnp.zeros((8, 128), f32)], axis=0)
        matrix[0:128, at] = tap_matrix(weights, tap, 1).astype(bf16)
        matrix[128:144, at] = skip_part.astype(bf16)
    total = jnp.zeros((144, SLAB), f32)
    for k_z in range(3):
        total = total + jnp.dot(
            matrix[:, k_z * 1152 : k_z * 1152 + 1152],
            unfolded[:, (2 - k_z) * FINE : (2 - k_z) * FINE + SLAB],
            preferred_element_type=f32,
        )
    skip_grad[...] = total[128:136].astype(bf16)
    own = joined[...].astype(f32)
    for tap in range(9):
        moved = fine_shift(own, tap // 3 - 1, tap % 3 - 1).astype(bf16)
        for k_z in range(3):
            at = (k_z * 9 + tap) * 16
            own_cols[at : at + 16, :] = moved[:, k_z * FINE : k_z * FINE + SLAB]
    d_up = jnp.concatenate([total[:128, :FINE], total[:128, FINE:]], axis=0).astype(bf16)
    parted = jnp.dot(d_up, interleave_matrix(True), preferred_element_type=f32)
    for y_par in (0, 1):
        for x_par in (0, 1):
            at = (y_par * 2 + x_par) * COARSE
            source = jnp.concatenate(
                [parted[:128, at : at + COARSE], parted[128:, at : at + COARSE]], axis=1
            )
            for k_y, y_off in PARITY[y_par]:
                for k_x, x_off in PARITY[x_par]:
                    tap = k_y * 3 + k_x
                    spread[tap * 128 : tap * 128 + 128, :] = coarse_shift(
                        source, -y_off, -x_off
                    ).astype(bf16)
    for tap in range(27):
        at = (tap // 9) * 1152 + (tap % 9) * 128
        up_matrix[:, at : at + 128] = up_weight[tap]
    low_plane, high_plane = spread[:, :COARSE], spread[:, COARSE:]
    coarse_own[...] = jnp.dot(
        up_matrix[:, 1152:2304], low_plane, preferred_element_type=f32
    ) + jnp.dot(up_matrix[:, 2304:], high_plane, preferred_element_type=f32)
    coarse_next[...] = jnp.dot(up_matrix[:, :1152], high_plane, preferred_element_type=f32)
    last = (((1,), (1,)), ((), ()))
    here, following = coarse[0], coarse[1]
    for k_z, source, plane in ((0, following, high_plane), (1, here, low_plane), (2, here, high_plane)):
        product = lax.dot_general(source, plane, last, preferred_element_type=f32)
        for tap in range(9):
            at = (k_z * 9 + tap) * 16
            weight_grads[at : at + 16, :] = product[:, tap * 128 : tap * 128 + 128].astype(bf16)
    weight_grads[432:864, :] = lax.dot_general(
        own_cols[...], grads[...], last, preferred_element_type=f32
    ).astype(bf16)
    rest = jnp.concatenate([second_grad[...], jnp.zeros((GRAD_ROWS - 1080, 128), f32)], axis=0)
    weight_grads[864:, :] = rest.astype(bf16)


def grad_sum_kernel(place, parts, spread):
    total = jnp.sum(parts[...].astype(f32), axis=0) * (1.0 / math.sqrt(SLAB))
    spread[...] = jnp.broadcast_to(total.astype(bf16)[None], spread.shape)


def grad_split_kernel(place, gathered, up, first_up, first_skip, second):
    values = gathered[...].reshape(GRAD_ROWS, 128).astype(f32)
    up[...] = values[:432].reshape(27, 16, 128)
    first = values[432:864].reshape(27, 16, 128)
    first_up[...] = first[:, :8]
    first_skip[...] = first[:, 8:]
    second[...] = values[864:1080].reshape(27, 8, 128)


def local(coarse, encoder_skip, up_weight, first_up, first_skip, second_weight, cotangent):
    slabs, shares = lax.axis_size("gz"), lax.axis_size("ch")
    place = jnp.stack([lax.axis_index("gz"), lax.axis_index("ch")]).astype(jnp.int32)
    upward = [(i, i + 1) for i in range(slabs - 1)]
    downward = [(i + 1, i) for i in range(slabs - 1)]

    def from_below(block):
        return lax.ppermute(block, "gz", upward)

    def from_above(block):
        return lax.ppermute(block, "gz", downward)

    def swap(block, axis):
        return lax.all_to_all(block, axis, 0, 0, tiled=True)

    def io_major(weight):
        return jnp.transpose(weight, (0, 2, 1))

    up_own, up_first = io_major(up_weight), io_major(first_up)
    skip_first, second_own = io_major(first_skip), io_major(second_weight)
    kernels = lax.all_gather(jnp.concatenate([second_own, up_first], axis=1), "ch", axis=0)

    here = coarse.reshape(16, COARSE)
    before, after = from_below(here), from_above(here)
    skip_low, skip_high = from_below(encoder_skip[:, 1]), from_above(encoder_skip[:, 0])
    cot_low, cot_high = from_below(cotangent[:, 1]), from_above(cotangent[:, 0])
    pieces = jnp.transpose(up_weight.reshape(27, 16, 8, 16), (1, 3, 0, 2)).reshape(16, 16, 216)
    pieces = jnp.pad(pieces, ((0, 0), (0, 0), (0, 40)))
    planes = jnp.concatenate([before, here, after], axis=1)
    planes = jnp.broadcast_to(planes[None], (shares, 16, 3 * COARSE))
    mixed = swap(jnp.concatenate([pieces, planes], axis=2), "ch")

    partial, joined = call(
        up_kernel,
        [((16, 8, SLAB), f32), ((16, HALOED), bf16)],
        (place, mixed, encoder_skip.reshape(8, SLAB), skip_low, skip_high, up_first, skip_first),
        [pltpu.VMEM((144, HALOED), bf16)],
    )
    pre, low, high, stats = call(
        first_sum_kernel,
        [((8, SLAB), f32), ((8, FINE), f32), ((8, FINE), f32), ((slabs, 8, 128), f32)],
        (place, swap(partial, "ch")),
    )
    (packed,) = call(
        first_norm_kernel,
        [((16, 16, 2 * SLAB + 128), bf16)],
        (
            place, pre, from_below(high), from_above(low), swap(stats, "gz"),
            cotangent.reshape(8, SLAB), cot_low, cot_high,
        ),
    )
    packed = swap(packed, "ch")
    unfolded = pltpu.VMEM((1152, HALOED), bf16)
    second_pre, low, high, stats = call(
        second_conv_kernel,
        [((128, SLAB), f32), ((128, FINE), bf16), ((128, FINE), bf16), ((slabs, 8, 128), f32)],
        (place, packed, kernels),
        [unfolded, pltpu.VMEM((128, 3456), bf16)],
    )
    decoded, normed, slope, inverse, sums = call(
        second_norm_kernel,
        [
            ((8, SLAB), bf16), ((128, HALOED), f32), ((128, HALOED), f32), ((8, 128), f32),
            ((slabs, 8, 128), f32),
        ],
        (place, second_pre, from_below(high), from_above(low), swap(stats, "gz"), packed),
    )
    low, high, slope_one, sums, second_grad = call(
        second_back_kernel,
        [
            ((128, FINE), bf16), ((128, FINE), bf16), ((128, SLAB), f32), ((slabs, 8, 128), f32),
            ((216, 128), f32),
        ],
        (place, normed, slope, inverse, swap(sums, "gz"), packed, kernels),
        [
            unfolded, pltpu.VMEM((128, 3456), bf16), pltpu.VMEM((128, SLAB), bf16),
            pltpu.VMEM((3, 128, 128), f32), pltpu.VMEM((216, SLAB), f32),
        ],
    )
    skip_grad, coarse_own, coarse_next, weight_grads = call(
        first_back_kernel,
        [((8, SLAB), bf16), ((16, COARSE), f32), ((16, COARSE), f32), ((GRAD_ROWS, 128), bf16)],
        (
            place, slope_one, from_below(high), from_above(low), swap(sums, "gz"), packed, kernels,
            skip_first, up_own, jnp.stack([here, after]), joined, second_grad,
        ),
        [
            unfolded, pltpu.VMEM((144, 3456), bf16), pltpu.VMEM((128, SLAB), bf16),
            pltpu.VMEM((3, 128, 128), f32), pltpu.VMEM((432, SLAB), bf16),
            pltpu.VMEM((1152, 2 * COARSE), bf16), pltpu.VMEM((16, 3456), bf16),
        ],
    )
    coarse_grad = (coarse_own + from_below(coarse_next)).astype(bf16)
    rows = GRAD_ROWS // slabs
    (spread,) = call(
        grad_sum_kernel,
        [((slabs, rows, 128), bf16)],
        (place, swap(weight_grads.reshape(slabs, rows, 128), "gz")),
    )
    grads = call(
        grad_split_kernel,
        [((27, 16, 128), f32), ((27, 8, 128), f32), ((27, 8, 128), f32), ((27, 8, 128), f32)],
        (place, swap(spread, "gz")),
    )
    grads = [jnp.transpose(grad, (0, 2, 1)) for grad in grads]
    return (
        decoded.reshape(8, 2, FINE),
        coarse_grad.reshape(16, 1, COARSE),
        skip_grad.reshape(8, 2, FINE),
        *grads,
    )


def solution(mesh):
    volume, kernel = P("ch", "gz", None), P(None, None, "ch")
    return jax.shard_map(
        local,
        mesh=mesh,
        in_specs=(volume, volume, kernel, kernel, kernel, kernel, volume),
        out_specs=(volume, volume, volume, kernel, kernel, kernel, kernel),
        check_vma=False,
    )
```

```python
import math

import jax
import jax.numpy as jnp
from jax import lax
from jax.experimental import pallas as pl
from jax.experimental.pallas import tpu as pltpu
from jax.sharding import PartitionSpec as P

C_OUT = 128
XC = 16
YC = 8
COARSE = YC * XC
FINE = 4 * COARSE
SLAB = 2 * FINE
HALOED = 4 * FINE
LEAK_SLOPE = 0.01
KINK_WIDTH = 0.01
NORM_EPS = 1e-05
PARITY = (((1, 0),), ((2, 0), (0, 1)))
GRAD_ROWS = 1280

f32 = jnp.float32
bf16 = jnp.bfloat16


def activate(u):
    q = u * u + KINK_WIDTH
    return 0.5 * (1.0 + LEAK_SLOPE) * u + 0.5 * (1.0 - LEAK_SLOPE) * (q * lax.rsqrt(q))


def activate_slope(u):
    return 0.5 * (1.0 + LEAK_SLOPE) + 0.5 * (1.0 - LEAK_SLOPE) * (
        u * lax.rsqrt(u * u + KINK_WIDTH)
    )


def shift(values, step_y, step_x, rows, columns):
    if step_y == 0 and step_x == 0:
        return values
    extent = values.shape[-1]
    cell = lax.broadcasted_iota(jnp.int32, (1, extent), 1)
    column = cell % columns + step_x
    row = cell // columns % rows + step_y
    inside = (column >= 0) & (column < columns) & (row >= 0) & (row < rows)
    moved = pltpu.roll(values, (-(step_y * columns + step_x)) % extent, 1)
    return moved * jnp.where(inside, 1.0, 0.0)


def fine_shift(values, step_y, step_x):
    return shift(values, step_y, step_x, 2 * YC, 2 * XC)


def coarse_shift(values, step_y, step_x):
    return shift(values, step_y, step_x, YC, XC)


def interleave_matrix(transposed):
    fine_dim = 0 if transposed else 1
    cell = lax.broadcasted_iota(jnp.int32, (FINE, FINE), fine_dim)
    other = lax.broadcasted_iota(jnp.int32, (FINE, FINE), 1 - fine_dim)
    y, x = cell // (2 * XC), cell % (2 * XC)
    source = ((y % 2) * 2 + x % 2) * COARSE + (y // 2) * XC + x // 2
    return jnp.where(source == other, 1.0, 0.0).astype(bf16)


def edge_mask(slab, slabs):
    plane = lax.broadcasted_iota(jnp.int32, (1, HALOED), 1) // FINE
    outside = ((plane == 0) & (slab == 0)) | ((plane == 3) & (slab == slabs - 1))
    return jnp.where(outside, 0.0, 1.0)


def as_row(column):
    return jnp.transpose(jnp.broadcast_to(column, (C_OUT, C_OUT)))[:1]


def as_column(row):
    return jnp.transpose(jnp.broadcast_to(row, (C_OUT, C_OUT)))[:, :1]


def call(kernel, outs, args, scratch=(), megabytes=8):
    specs = [pl.BlockSpec(memory_space=pltpu.SMEM)]
    specs += [pl.BlockSpec(memory_space=pltpu.VMEM)] * (len(args) - 1)
    return pl.pallas_call(
        kernel,
        out_shape=[jax.ShapeDtypeStruct(shape, dtype) for shape, dtype in outs],
        in_specs=specs,
        out_specs=[pl.BlockSpec(memory_space=pltpu.VMEM)] * len(outs),
        scratch_shapes=list(scratch),
        compiler_params=pltpu.CompilerParams(vmem_limit_bytes=megabytes * 2**20),
    )(*args)


def halo_kernel(place, coarse, skip, cotangent, upward, downward, own_skip, own_cot):
    cells = coarse[...].astype(f32)
    cells = [cells[:8], cells[8:]]
    skip_planes, cot_planes = skip[...].astype(f32), cotangent[...].astype(f32)
    last = cells + [skip_planes[:, 1], cot_planes[:, 1]]
    first = cells + [skip_planes[:, 0], cot_planes[:, 0]]
    upward[...] = jnp.concatenate(last, axis=1).astype(bf16)
    downward[...] = jnp.concatenate(first, axis=1).astype(bf16)
    own_skip[...] = jnp.concatenate([skip_planes[:, 0], skip_planes[:, 1]], axis=1).astype(bf16)
    own_cot[...] = jnp.concatenate([cot_planes[:, 0], cot_planes[:, 1]], axis=1).astype(bf16)


def mix_kernel(place, pieces, coarse, low, high, own_cot, mixed, pair, cot_planes):
    below, above = low[...].astype(f32), high[...].astype(f32)
    here = coarse[...].astype(f32)
    before = jnp.concatenate([below[:, :COARSE], below[:, COARSE : 2 * COARSE]], axis=0)
    after = jnp.concatenate([above[:, :COARSE], above[:, COARSE : 2 * COARSE]], axis=0)
    planes = jnp.concatenate([before, here, after], axis=1).astype(bf16)
    mixed[:, :, :256] = jnp.zeros((16, 16, 256), bf16)
    for target in range(16):
        mixed[target, :, :216] = pieces[target]
        mixed[target, :, 256:] = planes
    pair[0] = coarse[...]
    pair[1] = after.astype(bf16)
    cot = own_cot[...].astype(f32)
    lower = jnp.concatenate([below[:, 2 * COARSE + FINE :], cot[:, :FINE]], axis=1)
    upper = jnp.concatenate([cot[:, FINE:], above[:, 2 * COARSE + FINE :]], axis=1)
    cot_planes[0:16] = jnp.concatenate([lower, upper], axis=0).astype(bf16)
    cot_planes[16:32] = jnp.zeros((16, SLAB), bf16)


def up_kernel(place, mixed, own_skip, low, high, first_up, first_skip, partial, joined, unfolded):
    slab = place[0]
    packed = mixed[...]
    weights = packed[:, :, :256].reshape(256, 256)
    mixture = []
    for plane in range(3):
        source = packed[:, :, 256 + plane * COARSE : 256 + (plane + 1) * COARSE].reshape(256, COARSE)
        mixture.append(
            lax.dot_general(weights, source, (((0,), (0,)), ((), ())), preferred_element_type=f32)
        )
    rows = []
    for sources in (((2, 0), (0, 1)), ((1, 1),), ((2, 1), (0, 2)), ((1, 2),)):
        cells = []
        for y_par in (0, 1):
            for x_par in (0, 1):
                total = None
                for k_z, plane in sources:
                    for k_y, y_off in PARITY[y_par]:
                        for k_x, x_off in PARITY[x_par]:
                            tap = k_z * 9 + k_y * 3 + k_x
                            term = coarse_shift(mixture[plane][tap * 8 : tap * 8 + 8], y_off, x_off)
                            total = term if total is None else total + term
                cells.append(total)
        rows.append(jnp.concatenate(cells, axis=1))
    spread = jnp.concatenate(rows, axis=0).astype(bf16)
    fine = jnp.dot(spread, interleave_matrix(False), preferred_element_type=f32)
    first_inside = jnp.where(slab == 0, 0.0, 1.0)
    upsampled = jnp.concatenate(
        [fine[0:8] * first_inside, fine[8:16], fine[16:24], fine[24:32]], axis=1
    )
    skip_at = slice(2 * COARSE, 2 * COARSE + FINE)
    skip = jnp.concatenate(
        [low[:, skip_at].astype(f32), own_skip[...].astype(f32), high[:, skip_at].astype(f32)], axis=1
    )
    features = jnp.concatenate([upsampled, skip], axis=0)
    joined[...] = features.astype(bf16)
    for tap in range(9):
        unfolded[tap * 16 : tap * 16 + 16, :] = fine_shift(features, tap // 3 - 1, tap % 3 - 1).astype(bf16)
    total = jnp.zeros((C_OUT, SLAB), f32)
    for k_z in range(3):
        matrix = []
        for tap in range(9):
            up_part = first_up[k_z * 9 + tap].astype(f32)
            skip_part = first_skip[k_z * 9 + tap].astype(f32)
            matrix.append(jnp.concatenate([up_part, skip_part], axis=0))
        matrix = jnp.concatenate(matrix, axis=0).astype(bf16)
        total = total + lax.dot_general(
            matrix,
            unfolded[:, k_z * FINE : k_z * FINE + SLAB],
            (((0,), (0,)), ((), ())),
            preferred_element_type=f32,
        )
    partial[...] = total.reshape(16, 8, SLAB)


def in_parts(values):
    high = values.astype(bf16).astype(f32)
    middle = (values - high).astype(bf16).astype(f32)
    rest = values - high - middle
    lane = lax.broadcasted_iota(jnp.int32, (values.shape[0], 128), 1)
    return jnp.where(
        lane == 0, high, jnp.where(lane == 1, middle, jnp.where(lane == 2, rest, 0.0))
    )


def first_sum_kernel(place, parts, pre, stats):
    total = jnp.sum(parts[...], axis=0)
    pre[...] = total
    mean = jnp.sum(total, axis=1, keepdims=True) / SLAB
    deviation = total - mean
    square = jnp.sum(deviation * deviation, axis=1, keepdims=True)
    tail = in_parts(jnp.concatenate([mean, square], axis=0))
    half = FINE // 2
    first = jnp.concatenate([deviation[:, :half], deviation[:, half:FINE]], axis=0)
    last = jnp.concatenate([deviation[:, FINE : FINE + half], deviation[:, FINE + half :]], axis=0)
    first = jnp.concatenate([first, tail], axis=1).astype(bf16)
    last = jnp.concatenate([last, tail], axis=1).astype(bf16)
    for target in range(stats.shape[0]):
        above = target > place[0]

        @pl.when(above)
        def _():
            stats[target] = last

        @pl.when(jnp.logical_not(above))
        def _():
            stats[target] = first


def first_norm_kernel(place, pre, stats, packed):
    slab, slabs = place[0], stats.shape[0]
    half = FINE // 2
    tails = jnp.sum(stats[:, :, half:].astype(f32), axis=2, keepdims=True)
    means = tails[:, :8]
    mean = jnp.sum(means, axis=0) / slabs
    apart = means - mean[None]
    square = jnp.sum(tails[:, 8:] + SLAB * apart * apart, axis=0)
    inverse = lax.rsqrt(square / (slabs * SLAB) + NORM_EPS)

    def neighbour(index):
        block = stats[index].astype(f32)
        centre = jnp.sum(block[:8, half:], axis=1, keepdims=True)
        return jnp.concatenate([block[:8, :half], block[8:, :half]], axis=1) + centre

    low, high = neighbour(jnp.maximum(slab - 1, 0)), neighbour(jnp.minimum(slab + 1, slabs - 1))
    lower = jnp.concatenate([low, pre[:, :FINE]], axis=1)
    upper = jnp.concatenate([pre[:, FINE:], high], axis=1)
    wide = jnp.broadcast_to(inverse, (8, 128))
    main = wide.astype(bf16).astype(f32)
    block = jnp.concatenate(
        [
            jnp.concatenate([(lower - mean) * inverse, main], axis=1),
            jnp.concatenate([(upper - mean) * inverse, wide - main], axis=1),
        ],
        axis=0,
    ).astype(bf16)
    for target in range(16):
        packed[target] = block


def read_planes(packed, block):
    pair = packed[pl.ds(2 * block, 2), 0:16, :SLAB].astype(f32)
    return jnp.concatenate([pair[:, :8].reshape(16, SLAB), pair[:, 8:].reshape(16, SLAB)], axis=1)


def unfold_block(values, unfolded, block, sign):
    for tap in range(9):
        moved = fine_shift(values, sign * (tap // 3 - 1), sign * (tap % 3 - 1))
        unfolded[pl.ds(pl.multiple_of(tap * 128 + block * 16, 16), 16), :] = moved.astype(bf16)


def tap_matrix(weights, tap, first):
    both = weights[:, tap].astype(f32)
    return both[:, first * 8 : first * 8 + 8].reshape(C_OUT, C_OUT)


def second_conv_kernel(place, packed, weights, pre, low, high, stats, unfolded, matrix):
    mask = edge_mask(place[0], stats.shape[0])

    def prepare(block, carry):
        hidden = activate(read_planes(packed, block)).astype(bf16).astype(f32) * mask
        unfold_block(hidden, unfolded, block, 1)
        return carry

    lax.fori_loop(0, 8, prepare, 0)
    for tap in range(27):
        matrix[:, tap * 128 : tap * 128 + 128] = jnp.transpose(tap_matrix(weights, tap, 0)).astype(bf16)
    total = jnp.zeros((C_OUT, SLAB), f32)
    for k_z in range(3):
        total = total + jnp.dot(
            matrix[:, k_z * 1152 : k_z * 1152 + 1152],
            unfolded[:, k_z * FINE : k_z * FINE + SLAB],
            preferred_element_type=f32,
        )
    pre[...] = total
    mean = jnp.sum(total, axis=1, keepdims=True) / SLAB
    deviation = total - mean
    square = jnp.sum(deviation * deviation, axis=1, keepdims=True)
    low[...] = deviation[:, :FINE].astype(bf16)
    high[...] = deviation[:, FINE:].astype(bf16)
    row = lax.broadcasted_iota(jnp.int32, (8, 128), 0)
    tile = jnp.where(row < 4, as_row(mean), as_row(square))
    stats[...] = jnp.broadcast_to(tile[None], stats.shape)


def second_norm_kernel(
    place, pre, low, high, stats, cotangent, decoded, normed, slope, inverse_out, sums
):
    slab, share = place[0], place[1]
    slabs = stats.shape[0]
    gathered = stats[...]
    means = gathered[:, 0:1]
    mean_row = jnp.sum(means, axis=0) / slabs
    apart = means - mean_row[None]
    square = jnp.sum(gathered[:, 7:8] + SLAB * apart * apart, axis=0)
    inverse_row = lax.rsqrt(square / (slabs * SLAB) + NORM_EPS)
    inverse_out[...] = jnp.broadcast_to(inverse_row, inverse_out.shape)
    below = stats[jnp.maximum(slab - 1, 0)][0:1] - mean_row
    above = stats[jnp.minimum(slab + 1, slabs - 1)][0:1] - mean_row
    mean, inverse = as_column(mean_row), as_column(inverse_row)
    normed[:, :FINE] = (low[...].astype(f32) + as_column(below)) * inverse
    normed[:, FINE : 3 * FINE] = (pre[...] - mean) * inverse
    normed[:, 3 * FINE :] = (high[...].astype(f32) + as_column(above)) * inverse
    own = normed[pl.ds(pl.multiple_of(share * 8, 8), 8), FINE : 3 * FINE]
    decoded[...] = activate(own).astype(bf16)

    def prepare(block, carry):
        at = pl.ds(pl.multiple_of(block * 16, 16), 16)
        slope[at, :] = read_planes(cotangent, block) * activate_slope(normed[at, :])
        return carry

    lax.fori_loop(0, 8, prepare, 0)
    inner = slope[:, FINE : 3 * FINE]
    one = as_row(jnp.sum(inner, axis=1, keepdims=True))
    two = as_row(jnp.sum(inner * normed[:, FINE : 3 * FINE], axis=1, keepdims=True))
    row = lax.broadcasted_iota(jnp.int32, (8, 128), 0)
    sums[...] = jnp.broadcast_to(jnp.where(row < 4, one, two)[None], sums.shape)


def total_means(sums):
    totals = jnp.sum(sums[...], axis=0) / (sums.shape[0] * SLAB)
    return as_column(totals[0:1]), as_column(totals[7:8])


def second_back_kernel(
    place, normed, slope, inverse_row, sums_in, packed, weights,
    low, high, slope_one, sums, weight_grad, unfolded, matrix, grads, columns, own_cols,
):
    slab, share = place[0], place[1]
    mask = edge_mask(slab, sums.shape[0])
    mean_grad, mean_cross = total_means(sums_in)
    columns[0] = jnp.broadcast_to(mean_grad, (C_OUT, 128))
    columns[1] = jnp.broadcast_to(mean_cross, (C_OUT, 128))
    columns[2] = jnp.broadcast_to(as_column(inverse_row[0:1]), (C_OUT, 128))

    def prepare(block, carry):
        at = pl.ds(pl.multiple_of(block * 16, 16), 16)
        grad = columns[2, at, :1] * (slope[at, :] - columns[0, at, :1] - normed[at, :] * columns[1, at, :1])
        grad = grad.astype(bf16).astype(f32) * mask
        grads[at, :] = grad[:, FINE : 3 * FINE].astype(bf16)
        unfold_block(grad, unfolded, block, -1)
        return carry

    lax.fori_loop(0, 8, prepare, 0)
    for tap in range(27):
        matrix[:, tap * 128 : tap * 128 + 128] = tap_matrix(weights, tap, 0).astype(bf16)
    total = jnp.zeros((C_OUT, SLAB), f32)
    for k_z in range(3):
        total = total + jnp.dot(
            matrix[:, k_z * 1152 : k_z * 1152 + 1152],
            unfolded[:, (2 - k_z) * FINE : (2 - k_z) * FINE + SLAB],
            preferred_element_type=f32,
        )
    low[...] = total[:, :FINE].astype(bf16)
    high[...] = total[:, FINE:].astype(bf16)
    both = packed[:, :, :SLAB].astype(f32)
    first_normed = jnp.concatenate(
        [both[:, :8, FINE:].reshape(C_OUT, FINE), both[:, 8:, :FINE].reshape(C_OUT, FINE)], axis=1
    )
    inner = total * activate_slope(first_normed)
    slope_one[...] = inner
    one = as_row(jnp.sum(inner, axis=1, keepdims=True))
    two = as_row(jnp.sum(inner * first_normed, axis=1, keepdims=True))
    row = lax.broadcasted_iota(jnp.int32, (8, 128), 0)
    sums[...] = jnp.broadcast_to(jnp.where(row < 4, one, two)[None], sums.shape)
    own = packed[share].astype(f32)
    own = jnp.concatenate([own[:8, :SLAB], own[8:, :SLAB]], axis=1)
    own = activate(own).astype(bf16).astype(f32) * mask
    for tap in range(9):
        moved = fine_shift(own, tap // 3 - 1, tap % 3 - 1)
        for k_z in range(3):
            at = (k_z * 9 + tap) * 8
            own_cols[at : at + 8, :] = moved[:, k_z * FINE : k_z * FINE + SLAB]
    weight_grad[...] = lax.dot_general(
        own_cols[...].astype(bf16), grads[...], (((1,), (1,)), ((), ())), preferred_element_type=f32
    )


def first_back_kernel(
    place, slope, low, high, sums_in, packed, weights, first_skip, up_weight, coarse, joined, second_grad,
    skip_grad, coarse_own, coarse_next, weight_grads,
    unfolded, matrix, grads, columns, own_cols, spread, up_matrix,
):
    slab = place[0]
    mask = edge_mask(slab, sums_in.shape[0])
    mean_grad, mean_cross = total_means(sums_in)
    columns[0] = jnp.broadcast_to(mean_grad, (C_OUT, 128))
    columns[1] = jnp.broadcast_to(mean_cross, (C_OUT, 128))
    wide = packed[:, :, SLAB:].astype(f32)
    columns[2] = (wide[:, :8] + wide[:, 8:]).reshape(C_OUT, 128)

    def prepare(block, carry):
        at = pl.ds(pl.multiple_of(block * 16, 16), 16)
        normed = read_planes(packed, block)
        bottom = low[at, :].astype(f32) * activate_slope(normed[:, :FINE])
        top = high[at, :].astype(f32) * activate_slope(normed[:, 3 * FINE :])
        inner = jnp.concatenate([bottom, slope[at, :], top], axis=1)
        grad = columns[2, at, :1] * (inner - columns[0, at, :1] - normed * columns[1, at, :1])
        grad = grad.astype(bf16).astype(f32) * mask
        grads[at, :] = grad[:, FINE : 3 * FINE].astype(bf16)
        unfold_block(grad, unfolded, block, -1)
        return carry

    lax.fori_loop(0, 8, prepare, 0)
    for tap in range(27):
        at = slice(tap * 128, tap * 128 + 128)
        skip_part = jnp.concatenate([first_skip[tap].astype(f32), jnp.zeros((8, 128), f32)], axis=0)
        matrix[0:128, at] = tap_matrix(weights, tap, 1).astype(bf16)
        matrix[128:144, at] = skip_part.astype(bf16)
    total = jnp.zeros((144, SLAB), f32)
    for k_z in range(3):
        total = total + jnp.dot(
            matrix[:, k_z * 1152 : k_z * 1152 + 1152],
            unfolded[:, (2 - k_z) * FINE : (2 - k_z) * FINE + SLAB],
            preferred_element_type=f32,
        )
    skip_grad[...] = total[128:136].astype(bf16)
    own = joined[...].astype(f32)
    for tap in range(9):
        moved = fine_shift(own, tap // 3 - 1, tap % 3 - 1).astype(bf16)
        for k_z in range(3):
            at = (k_z * 9 + tap) * 16
            own_cols[at : at + 16, :] = moved[:, k_z * FINE : k_z * FINE + SLAB]
    d_up = jnp.concatenate([total[:128, :FINE], total[:128, FINE:]], axis=0).astype(bf16)
    parted = jnp.dot(d_up, interleave_matrix(True), preferred_element_type=f32)
    for y_par in (0, 1):
        for x_par in (0, 1):
            at = (y_par * 2 + x_par) * COARSE
            source = jnp.concatenate(
                [parted[:128, at : at + COARSE], parted[128:, at : at + COARSE]], axis=1
            )
            for k_y, y_off in PARITY[y_par]:
                for k_x, x_off in PARITY[x_par]:
                    tap = k_y * 3 + k_x
                    spread[tap * 128 : tap * 128 + 128, :] = coarse_shift(
                        source, -y_off, -x_off
                    ).astype(bf16)
    for tap in range(27):
        at = (tap // 9) * 1152 + (tap % 9) * 128
        up_matrix[:, at : at + 128] = up_weight[tap]
    low_plane, high_plane = spread[:, :COARSE], spread[:, COARSE:]
    coarse_own[...] = jnp.dot(
        up_matrix[:, 1152:2304], low_plane, preferred_element_type=f32
    ) + jnp.dot(up_matrix[:, 2304:], high_plane, preferred_element_type=f32)
    coarse_next[...] = jnp.dot(up_matrix[:, :1152], high_plane, preferred_element_type=f32)
    last = (((1,), (1,)), ((), ()))
    here, following = coarse[0], coarse[1]
    for k_z, source, plane in ((0, following, high_plane), (1, here, low_plane), (2, here, high_plane)):
        product = lax.dot_general(source, plane, last, preferred_element_type=f32)
        for tap in range(9):
            at = (k_z * 9 + tap) * 16
            weight_grads[at : at + 16, :] = product[:, tap * 128 : tap * 128 + 128].astype(bf16)
    weight_grads[432:864, :] = lax.dot_general(
        own_cols[...], grads[...], last, preferred_element_type=f32
    ).astype(bf16)
    rest = jnp.concatenate([second_grad[...], jnp.zeros((GRAD_ROWS - 1080, 128), f32)], axis=0)
    weight_grads[864:, :] = rest.astype(bf16)


def grad_sum_kernel(place, parts, spread):
    total = jnp.sum(parts[...].astype(f32), axis=0) * (1.0 / math.sqrt(SLAB))
    spread[...] = jnp.broadcast_to(total.astype(bf16)[None], spread.shape)


def grad_split_kernel(place, gathered, up, first_up, first_skip, second):
    values = gathered[...].reshape(GRAD_ROWS, 128).astype(f32)
    up[...] = values[:432].reshape(27, 16, 128)
    first = values[432:864].reshape(27, 16, 128)
    first_up[...] = first[:, :8]
    first_skip[...] = first[:, 8:]
    second[...] = values[864:1080].reshape(27, 8, 128)


def local(coarse, encoder_skip, up_weight, first_up, first_skip, second_weight, cotangent):
    slabs, shares = lax.axis_size("gz"), lax.axis_size("ch")
    place = jnp.stack([lax.axis_index("gz"), lax.axis_index("ch")]).astype(jnp.int32)
    upward = [(i, i + 1) for i in range(slabs - 1)]
    downward = [(i + 1, i) for i in range(slabs - 1)]

    def from_below(block):
        return lax.ppermute(block, "gz", upward)

    def from_above(block):
        return lax.ppermute(block, "gz", downward)

    def swap(block, axis):
        return lax.all_to_all(block, axis, 0, 0, tiled=True)

    def io_major(weight):
        return jnp.transpose(weight, (0, 2, 1))

    up_own, up_first = io_major(up_weight), io_major(first_up)
    skip_first, second_own = io_major(first_skip), io_major(second_weight)
    kernels = lax.all_gather(jnp.concatenate([second_own, up_first], axis=1), "ch", axis=0)

    here = coarse.reshape(16, COARSE)
    halo = ((8, 2 * COARSE + 2 * FINE), bf16)
    upper, lower, own_skip, own_cot = call(
        halo_kernel,
        [halo, halo, ((8, SLAB), bf16), ((8, SLAB), bf16)],
        (place, here, encoder_skip, cotangent),
    )
    low, high = from_below(upper), from_above(lower)
    pieces = jnp.transpose(up_weight.reshape(27, 16, 8, 16), (1, 3, 0, 2)).reshape(16, 16, 216)
    mixed, pair, cot_planes = call(
        mix_kernel,
        [((16, 16, 640), bf16), ((2, 16, COARSE), bf16), ((32, SLAB), bf16)],
        (place, pieces, here, low, high, own_cot),
    )
    cot_planes = lax.all_gather(cot_planes, "ch", axis=0)

    partial, joined = call(
        up_kernel,
        [((16, 8, SLAB), f32), ((16, HALOED), bf16)],
        (place, swap(mixed, "ch"), own_skip, low, high, up_first, skip_first),
        [pltpu.VMEM((144, HALOED), bf16)],
    )
    pre, stats = call(
        first_sum_kernel,
        [((8, SLAB), f32), ((slabs, 16, FINE // 2 + 128), bf16)],
        (place, swap(partial, "ch")),
    )
    (packed,) = call(
        first_norm_kernel, [((16, 16, SLAB + 128), bf16)], (place, pre, swap(stats, "gz"))
    )
    packed = swap(packed, "ch")
    unfolded = pltpu.VMEM((1152, HALOED), bf16)
    second_pre, low, high, stats = call(
        second_conv_kernel,
        [((128, SLAB), f32), ((128, FINE), bf16), ((128, FINE), bf16), ((slabs, 8, 128), f32)],
        (place, packed, kernels),
        [unfolded, pltpu.VMEM((128, 3456), bf16)],
        16,
    )
    decoded, normed, slope, inverse, sums = call(
        second_norm_kernel,
        [
            ((8, SLAB), bf16), ((128, HALOED), f32), ((128, HALOED), f32), ((8, 128), f32),
            ((slabs, 8, 128), f32),
        ],
        (place, second_pre, from_below(high), from_above(low), swap(stats, "gz"), cot_planes),
    )
    low, high, slope_one, sums, second_grad = call(
        second_back_kernel,
        [
            ((128, FINE), bf16), ((128, FINE), bf16), ((128, SLAB), f32), ((slabs, 8, 128), f32),
            ((216, 128), f32),
        ],
        (place, normed, slope, inverse, swap(sums, "gz"), packed, kernels),
        [
            unfolded, pltpu.VMEM((128, 3456), bf16), pltpu.VMEM((128, SLAB), bf16),
            pltpu.VMEM((3, 128, 128), f32), pltpu.VMEM((216, SLAB), f32),
        ],
        16,
    )
    skip_grad, coarse_own, coarse_next, weight_grads = call(
        first_back_kernel,
        [((8, SLAB), bf16), ((16, COARSE), f32), ((16, COARSE), f32), ((GRAD_ROWS, 128), bf16)],
        (
            place, slope_one, from_below(high), from_above(low), swap(sums, "gz"), packed, kernels,
            skip_first, up_own, pair, joined, second_grad,
        ),
        [
            unfolded, pltpu.VMEM((144, 3456), bf16), pltpu.VMEM((128, SLAB), bf16),
            pltpu.VMEM((3, 128, 128), f32), pltpu.VMEM((432, SLAB), bf16),
            pltpu.VMEM((1152, 2 * COARSE), bf16), pltpu.VMEM((16, 3456), bf16),
        ],
        20,
    )
    coarse_grad = (coarse_own + from_below(coarse_next)).astype(bf16)
    rows = GRAD_ROWS // slabs
    (spread,) = call(
        grad_sum_kernel,
        [((slabs, rows, 128), bf16)],
        (place, swap(weight_grads.reshape(slabs, rows, 128), "gz")),
    )
    grads = call(
        grad_split_kernel,
        [((27, 16, 128), f32), ((27, 8, 128), f32), ((27, 8, 128), f32), ((27, 8, 128), f32)],
        (place, swap(spread, "gz")),
    )
    grads = [jnp.transpose(grad, (0, 2, 1)) for grad in grads]
    return (
        decoded.reshape(8, 2, FINE),
        coarse_grad.reshape(16, 1, COARSE),
        skip_grad.reshape(8, 2, FINE),
        *grads,
    )


def solution(mesh):
    volume, kernel = P("ch", "gz", None), P(None, None, "ch")
    return jax.shard_map(
        local,
        mesh=mesh,
        in_specs=(volume, volume, kernel, kernel, kernel, kernel, volume),
        out_specs=(volume, volume, volume, kernel, kernel, kernel, kernel),
        check_vma=False,
    )
```

```python
import math

import jax
import jax.numpy as jnp
from jax import lax
from jax.experimental import pallas as pl
from jax.experimental.pallas import tpu as pltpu
from jax.sharding import PartitionSpec as P

C_OUT = 128
XC = 16
YC = 8
COARSE = YC * XC
FINE = 4 * COARSE
SLAB = 2 * FINE
HALOED = 4 * FINE
LEAK_SLOPE = 0.01
KINK_WIDTH = 0.01
NORM_EPS = 1e-05
PARITY = (((1, 0),), ((2, 0), (0, 1)))
GRAD_ROWS = 1280

f32 = jnp.float32
bf16 = jnp.bfloat16


def activate(u):
    q = u * u + KINK_WIDTH
    return 0.5 * (1.0 + LEAK_SLOPE) * u + 0.5 * (1.0 - LEAK_SLOPE) * (q * lax.rsqrt(q))


def activate_slope(u):
    return 0.5 * (1.0 + LEAK_SLOPE) + 0.5 * (1.0 - LEAK_SLOPE) * (
        u * lax.rsqrt(u * u + KINK_WIDTH)
    )


def shift(values, step_y, step_x, rows, columns):
    if step_y == 0 and step_x == 0:
        return values
    extent = values.shape[-1]
    cell = lax.broadcasted_iota(jnp.int32, (1, extent), 1)
    column = cell % columns + step_x
    row = cell // columns % rows + step_y
    inside = (column >= 0) & (column < columns) & (row >= 0) & (row < rows)
    moved = pltpu.roll(values, (-(step_y * columns + step_x)) % extent, 1)
    return moved * jnp.where(inside, 1.0, 0.0)


def fine_shift(values, step_y, step_x):
    return shift(values, step_y, step_x, 2 * YC, 2 * XC)


def coarse_shift(values, step_y, step_x):
    return shift(values, step_y, step_x, YC, XC)


def interleave_matrix(transposed):
    fine_dim = 0 if transposed else 1
    cell = lax.broadcasted_iota(jnp.int32, (FINE, FINE), fine_dim)
    other = lax.broadcasted_iota(jnp.int32, (FINE, FINE), 1 - fine_dim)
    y, x = cell // (2 * XC), cell % (2 * XC)
    source = ((y % 2) * 2 + x % 2) * COARSE + (y // 2) * XC + x // 2
    return jnp.where(source == other, 1.0, 0.0).astype(bf16)


def edge_mask(slab, slabs):
    plane = lax.broadcasted_iota(jnp.int32, (1, HALOED), 1) // FINE
    outside = ((plane == 0) & (slab == 0)) | ((plane == 3) & (slab == slabs - 1))
    return jnp.where(outside, 0.0, 1.0)


def as_row(column):
    return jnp.transpose(jnp.broadcast_to(column, (C_OUT, C_OUT)))[:1]


def as_column(row):
    return jnp.transpose(jnp.broadcast_to(row, (C_OUT, C_OUT)))[:, :1]


def call(kernel, outs, args, scratch=(), megabytes=8, far=(), far_outs=(), near=(), near_outs=()):
    args = list(args)
    for index in far:
        args[index] = pltpu.with_memory_space_constraint(args[index], pltpu.HBM)
    for index in near:
        args[index] = pltpu.with_memory_space_constraint(args[index], pltpu.VMEM)

    def spec(index, which):
        return pl.BlockSpec(memory_space=pltpu.HBM if index in which else pltpu.VMEM)

    def out(index, shape, dtype):
        if index in far_outs:
            return pltpu.HBM(shape, dtype)
        return pltpu.VMEM(shape, dtype) if index in near_outs else jax.ShapeDtypeStruct(shape, dtype)

    return pl.pallas_call(
        kernel,
        out_shape=[out(index, *shape) for index, shape in enumerate(outs)],
        in_specs=[spec(index, far) for index in range(len(args))],
        out_specs=[spec(index, far_outs) for index in range(len(outs))],
        scratch_shapes=list(scratch),
        compiler_params=pltpu.CompilerParams(vmem_limit_bytes=megabytes * 2**20),
    )(*args)


def copies(sources, targets, semaphores):
    started = []
    for index, (source, target) in enumerate(zip(sources, targets)):
        copy = pltpu.make_async_copy(source, target, semaphores.at[index])
        copy.start()
        started.append(copy)
    return started


def halo_kernel(
    far_coarse, far_skip, far_cot, upward, downward, own_skip, own_cot, coarse, skip, cotangent, semaphores
):
    for copy in copies((far_coarse, far_skip, far_cot), (coarse, skip, cotangent), semaphores):
        copy.wait()
    cells = coarse[...].astype(f32)
    cells = [cells[:8], cells[8:]]
    skip_planes, cot_planes = skip[...].astype(f32), cotangent[...].astype(f32)
    last = cells + [skip_planes[:, 1], cot_planes[:, 1]]
    first = cells + [skip_planes[:, 0], cot_planes[:, 0]]
    upward[...] = jnp.concatenate(last, axis=1).astype(bf16)
    downward[...] = jnp.concatenate(first, axis=1).astype(bf16)
    own_skip[...] = jnp.concatenate([skip_planes[:, 0], skip_planes[:, 1]], axis=1).astype(bf16)
    own_cot[...] = jnp.concatenate([cot_planes[:, 0], cot_planes[:, 1]], axis=1).astype(bf16)


def mix_kernel(pieces, coarse, low, high, own_cot, mixed, pair, cot_planes):
    below, above = low[...].astype(f32), high[...].astype(f32)
    here = coarse[...].astype(f32)
    before = jnp.concatenate([below[:, :COARSE], below[:, COARSE : 2 * COARSE]], axis=0)
    after = jnp.concatenate([above[:, :COARSE], above[:, COARSE : 2 * COARSE]], axis=0)
    planes = jnp.concatenate([before, here, after], axis=1).astype(bf16)
    mixed[:, :, :256] = jnp.zeros((16, 16, 256), bf16)
    for target in range(16):
        mixed[target, :, :216] = pieces[target]
        mixed[target, :, 256:] = planes
    pair[0] = coarse[...]
    pair[1] = after.astype(bf16)
    cot = own_cot[...].astype(f32)
    lower = jnp.concatenate([below[:, 2 * COARSE + FINE :], cot[:, :FINE]], axis=1)
    upper = jnp.concatenate([cot[:, FINE:], above[:, 2 * COARSE + FINE :]], axis=1)
    cot_planes[0:16] = jnp.concatenate([lower, upper], axis=0).astype(bf16)
    cot_planes[16:32] = jnp.zeros((16, SLAB), bf16)


def up_kernel(mixed, own_skip, low, high, first_up, first_skip, partial, joined, unfolded):
    slab = lax.axis_index("gz")
    packed = mixed[...]
    weights = packed[:, :, :256].reshape(256, 256)
    mixture = []
    for plane in range(3):
        source = packed[:, :, 256 + plane * COARSE : 256 + (plane + 1) * COARSE].reshape(256, COARSE)
        mixture.append(
            lax.dot_general(weights, source, (((0,), (0,)), ((), ())), preferred_element_type=f32)
        )
    rows = []
    for sources in (((2, 0), (0, 1)), ((1, 1),), ((2, 1), (0, 2)), ((1, 2),)):
        cells = []
        for y_par in (0, 1):
            for x_par in (0, 1):
                total = None
                for k_z, plane in sources:
                    for k_y, y_off in PARITY[y_par]:
                        for k_x, x_off in PARITY[x_par]:
                            tap = k_z * 9 + k_y * 3 + k_x
                            term = coarse_shift(mixture[plane][tap * 8 : tap * 8 + 8], y_off, x_off)
                            total = term if total is None else total + term
                cells.append(total)
        rows.append(jnp.concatenate(cells, axis=1))
    spread = jnp.concatenate(rows, axis=0).astype(bf16)
    fine = jnp.dot(spread, interleave_matrix(False), preferred_element_type=f32)
    first_inside = jnp.where(slab == 0, 0.0, 1.0)
    upsampled = jnp.concatenate(
        [fine[0:8] * first_inside, fine[8:16], fine[16:24], fine[24:32]], axis=1
    )
    skip_at = slice(2 * COARSE, 2 * COARSE + FINE)
    skip = jnp.concatenate(
        [low[:, skip_at].astype(f32), own_skip[...].astype(f32), high[:, skip_at].astype(f32)], axis=1
    )
    features = jnp.concatenate([upsampled, skip], axis=0)
    joined[...] = features.astype(bf16)
    for tap in range(9):
        unfolded[tap * 16 : tap * 16 + 16, :] = fine_shift(features, tap // 3 - 1, tap % 3 - 1).astype(bf16)
    total = jnp.zeros((C_OUT, SLAB), f32)
    for k_z in range(3):
        matrix = []
        for tap in range(9):
            up_part = first_up[k_z * 9 + tap].astype(f32)
            skip_part = first_skip[k_z * 9 + tap].astype(f32)
            matrix.append(jnp.concatenate([up_part, skip_part], axis=0))
        matrix = jnp.concatenate(matrix, axis=0).astype(bf16)
        total = total + lax.dot_general(
            matrix,
            unfolded[:, k_z * FINE : k_z * FINE + SLAB],
            (((0,), (0,)), ((), ())),
            preferred_element_type=f32,
        )
    mean = jnp.sum(total, axis=1, keepdims=True) / SLAB
    deviation = total - mean
    first = jnp.concatenate([deviation[:, :FINE], in_parts(mean)], axis=1).reshape(16, 8, FINE + 128)
    second = jnp.concatenate([deviation[:, FINE:], jnp.zeros((C_OUT, 128), f32)], axis=1)
    partial[...] = jnp.concatenate([first, second.reshape(16, 8, FINE + 128)], axis=1).astype(bf16)


def in_parts(values):
    high = values.astype(bf16).astype(f32)
    middle = (values - high).astype(bf16).astype(f32)
    rest = values - high - middle
    lane = lax.broadcasted_iota(jnp.int32, (values.shape[0], 128), 1)
    return jnp.where(
        lane == 0, high, jnp.where(lane == 1, middle, jnp.where(lane == 2, rest, 0.0))
    )


def first_sum_kernel(parts, pre, stats):
    slab = lax.axis_index("gz")
    both = jnp.sum(parts[...].astype(f32), axis=0)
    total = jnp.concatenate([both[:8, :FINE], both[8:, :FINE]], axis=1)
    total = total + jnp.sum(both[:8, FINE:], axis=1, keepdims=True)
    pre[...] = total
    mean = jnp.sum(total, axis=1, keepdims=True) / SLAB
    deviation = total - mean
    square = jnp.sum(deviation * deviation, axis=1, keepdims=True)
    tail = in_parts(jnp.concatenate([mean, square], axis=0))
    half = FINE // 2
    first = jnp.concatenate([deviation[:, :half], deviation[:, half:FINE]], axis=0)
    last = jnp.concatenate([deviation[:, FINE : FINE + half], deviation[:, FINE + half :]], axis=0)
    first = jnp.concatenate([first, tail], axis=1).astype(bf16)
    last = jnp.concatenate([last, tail], axis=1).astype(bf16)
    for target in range(stats.shape[0]):
        above = target > slab

        @pl.when(above)
        def _():
            stats[target] = last

        @pl.when(jnp.logical_not(above))
        def _():
            stats[target] = first


def first_norm_kernel(pre, stats, packed):
    slab, slabs = lax.axis_index("gz"), stats.shape[0]
    half = FINE // 2
    tails = jnp.sum(stats[:, :, half:].astype(f32), axis=2, keepdims=True)
    means = tails[:, :8]
    mean = jnp.sum(means, axis=0) / slabs
    apart = means - mean[None]
    square = jnp.sum(tails[:, 8:] + SLAB * apart * apart, axis=0)
    inverse = lax.rsqrt(square / (slabs * SLAB) + NORM_EPS)

    def neighbour(index):
        block = stats[index].astype(f32)
        centre = jnp.sum(block[:8, half:], axis=1, keepdims=True)
        return jnp.concatenate([block[:8, :half], block[8:, :half]], axis=1) + centre

    low, high = neighbour(jnp.maximum(slab - 1, 0)), neighbour(jnp.minimum(slab + 1, slabs - 1))
    lower = jnp.concatenate([low, pre[:, :FINE]], axis=1)
    upper = jnp.concatenate([pre[:, FINE:], high], axis=1)
    wide = jnp.broadcast_to(inverse, (8, 128))
    main = wide.astype(bf16).astype(f32)
    block = jnp.concatenate(
        [
            jnp.concatenate([(lower - mean) * inverse, main], axis=1),
            jnp.concatenate([(upper - mean) * inverse, wide - main], axis=1),
        ],
        axis=0,
    ).astype(bf16)
    for target in range(16):
        packed[target] = block


def read_planes(packed, block):
    pair = packed[pl.ds(2 * block, 2), 0:16, :SLAB].astype(f32)
    return jnp.concatenate([pair[:, :8].reshape(16, SLAB), pair[:, 8:].reshape(16, SLAB)], axis=1)


def unfold_block(values, unfolded, block, sign):
    for tap in range(9):
        moved = fine_shift(values, sign * (tap // 3 - 1), sign * (tap % 3 - 1))
        unfolded[tap, pl.ds(pl.multiple_of(block * 16, 16), 16), :] = moved.astype(bf16)


def tap_matrix(weights, tap, first):
    both = weights[:, tap].astype(f32)
    return both[:, first * 8 : first * 8 + 8].reshape(C_OUT, C_OUT)


def matrix_kernel(weights, first_skip, forward, far_backward, far_first, backward, first, semaphores):
    for tap in range(27):
        at = slice(tap * 128, tap * 128 + 128)
        second = tap_matrix(weights, tap, 0)
        forward[:, at] = jnp.transpose(second).astype(bf16)
        backward[:, at] = second.astype(bf16)
        skip_part = jnp.concatenate([first_skip[tap].astype(f32), jnp.zeros((8, 128), f32)], axis=0)
        first[0:128, at] = tap_matrix(weights, tap, 1).astype(bf16)
        first[128:144, at] = skip_part.astype(bf16)
    for copy in copies((backward, first), (far_backward, far_first), semaphores):
        copy.wait()


def second_conv_kernel(
    packed, matrix, pre, low, high, stats, unfolded
):
    mask = edge_mask(lax.axis_index("gz"), stats.shape[0])

    def prepare(block, carry):
        hidden = activate(read_planes(packed, block)).astype(bf16).astype(f32) * mask
        unfold_block(hidden, unfolded, block, 1)
        return carry

    lax.fori_loop(0, 8, prepare, 0)
    total = jnp.zeros((C_OUT, SLAB), f32)
    for k_z in range(3):
        total = total + jnp.dot(
            matrix[:, k_z * 1152 : k_z * 1152 + 1152],
            unfolded[:, :, k_z * FINE : k_z * FINE + SLAB].reshape(1152, SLAB),
            preferred_element_type=f32,
        )
    pre[...] = total
    mean = jnp.sum(total, axis=1, keepdims=True) / SLAB
    deviation = total - mean
    square = jnp.sum(deviation * deviation, axis=1, keepdims=True)
    low[...] = deviation[:, :FINE].astype(bf16)
    high[...] = deviation[:, FINE:].astype(bf16)
    row = lax.broadcasted_iota(jnp.int32, (2, 128), 0)
    tile = jnp.where(row < 1, as_row(mean), as_row(square))
    stats[...] = jnp.broadcast_to(tile[None], stats.shape)


def second_norm_kernel(
    pre, low, high, stats, far_cot, decoded, normed, slope, inverse_out, sums, cotangent, semaphores
):
    (fetch,) = copies((far_cot.at[:, pl.ds(0, 16)],), (cotangent,), semaphores)
    slab, share = lax.axis_index("gz"), lax.axis_index("ch")
    slabs = stats.shape[0]
    gathered = stats[...]
    means = gathered[:, 0:1]
    mean_row = jnp.sum(means, axis=0) / slabs
    apart = means - mean_row[None]
    square = jnp.sum(gathered[:, 1:2] + SLAB * apart * apart, axis=0)
    inverse_row = lax.rsqrt(square / (slabs * SLAB) + NORM_EPS)
    inverse_out[...] = jnp.broadcast_to(inverse_row, inverse_out.shape)
    below = stats[jnp.maximum(slab - 1, 0)][0:1] - mean_row
    above = stats[jnp.minimum(slab + 1, slabs - 1)][0:1] - mean_row
    mean, inverse = as_column(mean_row), as_column(inverse_row)
    normed[:, :FINE] = (low[...].astype(f32) + as_column(below)) * inverse
    normed[:, 3 * FINE :] = (high[...].astype(f32) + as_column(above)) * inverse
    normed[:, FINE : 3 * FINE] = (pre[...] - mean) * inverse
    own = normed[pl.ds(pl.multiple_of(share * 8, 8), 8), FINE : 3 * FINE]
    decoded[...] = activate(own).astype(bf16)

    def prepare(block, carry):
        at = pl.ds(pl.multiple_of(block * 16, 16), 16)
        slope[at, :] = read_planes(cotangent, block) * activate_slope(normed[at, :])
        return carry

    fetch.wait()
    lax.fori_loop(0, 8, prepare, 0)
    inner = slope[:, FINE : 3 * FINE]
    one = as_row(jnp.sum(inner, axis=1, keepdims=True))
    two = as_row(jnp.sum(inner * normed[:, FINE : 3 * FINE], axis=1, keepdims=True))
    row = lax.broadcasted_iota(jnp.int32, (2, 128), 0)
    sums[...] = jnp.broadcast_to(jnp.where(row < 1, one, two)[None], sums.shape)


def total_means(sums):
    totals = jnp.sum(sums[...], axis=0) / (sums.shape[0] * SLAB)
    return as_column(totals[0:1]), as_column(totals[1:2])


def second_back_kernel(
    normed, slope, inverse_row, sums_in, packed, far_matrix,
    low, high, slope_one, sums, weight_grad,
    unfolded, grads, columns, matrix, own_unfolded, semaphores,
):
    (fetch,) = copies((far_matrix,), (matrix,), semaphores)
    slab, share = lax.axis_index("gz"), lax.axis_index("ch")
    mask = edge_mask(slab, sums.shape[0])
    mean_grad, mean_cross = total_means(sums_in)
    columns[0] = jnp.broadcast_to(mean_grad, (C_OUT, 128))
    columns[1] = jnp.broadcast_to(mean_cross, (C_OUT, 128))
    columns[2] = jnp.broadcast_to(as_column(inverse_row[0:1]), (C_OUT, 128))

    def prepare(block, carry):
        at = pl.ds(pl.multiple_of(block * 16, 16), 16)
        grad = columns[2, at, :1] * (slope[at, :] - columns[0, at, :1] - normed[at, :] * columns[1, at, :1])
        grad = grad.astype(bf16).astype(f32) * mask
        grads[at, :] = grad[:, FINE : 3 * FINE]
        unfold_block(grad, unfolded, block, -1)
        return carry

    lax.fori_loop(0, 8, prepare, 0)
    fetch.wait()
    total = jnp.zeros((C_OUT, SLAB), f32)
    for k_z in range(3):
        total = total + jnp.dot(
            matrix[:, k_z * 1152 : k_z * 1152 + 1152],
            unfolded[:, :, (2 - k_z) * FINE : (2 - k_z) * FINE + SLAB].reshape(1152, SLAB),
            preferred_element_type=f32,
        )
    low[...] = total[:, :FINE].astype(bf16)
    high[...] = total[:, FINE:].astype(bf16)
    both = packed[:, :, :SLAB].astype(f32)
    first_normed = jnp.concatenate(
        [both[:, :8, FINE:].reshape(C_OUT, FINE), both[:, 8:, :FINE].reshape(C_OUT, FINE)], axis=1
    )
    inner = total * activate_slope(first_normed)
    slope_one[...] = inner
    one = as_row(jnp.sum(inner, axis=1, keepdims=True))
    two = as_row(jnp.sum(inner * first_normed, axis=1, keepdims=True))
    row = lax.broadcasted_iota(jnp.int32, (2, 128), 0)
    sums[...] = jnp.broadcast_to(jnp.where(row < 1, one, two)[None], sums.shape)
    own = activate(read_planes(packed, share // 2)).astype(bf16).astype(f32) * mask
    for tap in range(9):
        own_unfolded[tap * 16 : tap * 16 + 16, :] = fine_shift(own, tap // 3 - 1, tap % 3 - 1).astype(bf16)
    odd = share % 2 == 1
    turned = jnp.transpose(grads[...]).astype(bf16)
    for k_z in range(3):
        product = jnp.dot(
            own_unfolded[:, k_z * FINE : k_z * FINE + SLAB], turned, preferred_element_type=f32
        ).reshape(9, 2, 8, 128)
        weight_grad[k_z * 72 : k_z * 72 + 72, :] = jnp.where(odd, product[:, 1], product[:, 0]).reshape(72, 128)


def first_back_kernel(
    slope, low, high, sums_in, packed, far_matrix, up_weight, coarse, joined, second_grad,
    skip_grad, coarse_own, coarse_next, weight_grads,
    unfolded, grads, columns, spread, up_matrix, matrix, own_unfolded, semaphores,
):
    (fetch,) = copies((far_matrix,), (matrix,), semaphores)
    slab = lax.axis_index("gz")
    mask = edge_mask(slab, sums_in.shape[0])
    mean_grad, mean_cross = total_means(sums_in)
    columns[0] = jnp.broadcast_to(mean_grad, (C_OUT, 128))
    columns[1] = jnp.broadcast_to(mean_cross, (C_OUT, 128))
    wide = packed[:, :, SLAB:].astype(f32)
    columns[2] = (wide[:, :8] + wide[:, 8:]).reshape(C_OUT, 128)

    def prepare(block, carry):
        at = pl.ds(pl.multiple_of(block * 16, 16), 16)
        normed = read_planes(packed, block)
        bottom = low[at, :].astype(f32) * activate_slope(normed[:, :FINE])
        top = high[at, :].astype(f32) * activate_slope(normed[:, 3 * FINE :])
        inner = jnp.concatenate([bottom, slope[at, :], top], axis=1)
        grad = columns[2, at, :1] * (inner - columns[0, at, :1] - normed * columns[1, at, :1])
        grad = grad.astype(bf16).astype(f32) * mask
        grads[at, :] = grad[:, FINE : 3 * FINE]
        unfold_block(grad, unfolded, block, -1)
        return carry

    lax.fori_loop(0, 8, prepare, 0)
    fetch.wait()
    total = jnp.zeros((144, SLAB), f32)
    for k_z in range(3):
        total = total + jnp.dot(
            matrix[:, k_z * 1152 : k_z * 1152 + 1152],
            unfolded[:, :, (2 - k_z) * FINE : (2 - k_z) * FINE + SLAB].reshape(1152, SLAB),
            preferred_element_type=f32,
        )
    skip_grad[...] = total[128:136].astype(bf16)
    d_up = jnp.concatenate([total[:128, :FINE], total[:128, FINE:]], axis=0).astype(bf16)
    last = (((1,), (1,)), ((), ()))
    parted = jnp.dot(d_up, interleave_matrix(True), preferred_element_type=f32)
    for y_par in (0, 1):
        for x_par in (0, 1):
            at = (y_par * 2 + x_par) * COARSE
            source = jnp.concatenate(
                [parted[:128, at : at + COARSE], parted[128:, at : at + COARSE]], axis=1
            )
            for k_y, y_off in PARITY[y_par]:
                for k_x, x_off in PARITY[x_par]:
                    tap = k_y * 3 + k_x
                    spread[tap * 128 : tap * 128 + 128, :] = coarse_shift(
                        source, -y_off, -x_off
                    ).astype(bf16)
    for tap in range(27):
        at = (tap // 9) * 1152 + (tap % 9) * 128
        up_matrix[:, at : at + 128] = up_weight[tap]
    low_plane, high_plane = spread[:, :COARSE], spread[:, COARSE:]
    coarse_own[...] = jnp.dot(
        up_matrix[:, 1152:2304], low_plane, preferred_element_type=f32
    ) + jnp.dot(up_matrix[:, 2304:], high_plane, preferred_element_type=f32)
    coarse_next[...] = jnp.dot(up_matrix[:, :1152], high_plane, preferred_element_type=f32)
    here, following = coarse[0], coarse[1]
    for k_z, source, plane in ((0, following, high_plane), (1, here, low_plane), (2, here, high_plane)):
        product = lax.dot_general(source, plane, last, preferred_element_type=f32)
        for tap in range(9):
            at = (k_z * 9 + tap) * 16
            weight_grads[at : at + 16, :] = product[:, tap * 128 : tap * 128 + 128].astype(bf16)
    own = joined[...].astype(f32)
    for tap in range(9):
        own_unfolded[tap * 16 : tap * 16 + 16, :] = fine_shift(own, tap // 3 - 1, tap % 3 - 1).astype(bf16)
    turned = jnp.transpose(grads[...]).astype(bf16)
    for k_z in range(3):
        product = jnp.dot(
            own_unfolded[:, k_z * FINE : k_z * FINE + SLAB], turned, preferred_element_type=f32
        )
        weight_grads[432 + k_z * 144 : 576 + k_z * 144, :] = product.astype(bf16)
    rest = jnp.concatenate([second_grad[...], jnp.zeros((GRAD_ROWS - 1080, 128), f32)], axis=0)
    weight_grads[864:, :] = rest.astype(bf16)


def grad_sum_kernel(parts, spread):
    total = jnp.sum(parts[...].astype(f32), axis=0) * (1.0 / math.sqrt(SLAB))
    spread[...] = jnp.broadcast_to(total.astype(bf16)[None], spread.shape)


def grad_split_kernel(gathered, up, first_up, first_skip, second):
    values = gathered[...].reshape(GRAD_ROWS, 128).astype(f32)
    up[...] = values[:432].reshape(27, 16, 128)
    first = values[432:864].reshape(27, 16, 128)
    first_up[...] = first[:, :8]
    first_skip[...] = first[:, 8:]
    second[...] = values[864:1080].reshape(27, 8, 128)


def local(coarse, encoder_skip, up_weight, first_up, first_skip, second_weight, cotangent):
    slabs, shares = lax.axis_size("gz"), lax.axis_size("ch")
    upward = [(i, i + 1) for i in range(slabs - 1)]
    downward = [(i + 1, i) for i in range(slabs - 1)]

    def from_below(block):
        return lax.ppermute(block, "gz", upward)

    def from_above(block):
        return lax.ppermute(block, "gz", downward)

    def swap(block, axis):
        return lax.all_to_all(block, axis, 0, 0, tiled=True)

    def io_major(weight):
        return jnp.transpose(weight, (0, 2, 1))

    up_own, up_first = io_major(up_weight), io_major(first_up)
    skip_first, second_own = io_major(first_skip), io_major(second_weight)

    here = coarse.reshape(16, COARSE)
    halo = ((8, 2 * COARSE + 2 * FINE), bf16)
    upper, lower, own_skip, own_cot = call(
        halo_kernel,
        [halo, halo, ((8, SLAB), bf16), ((8, SLAB), bf16)],
        (here, encoder_skip, cotangent),
        [
            pltpu.VMEM((16, COARSE), bf16), pltpu.VMEM((8, 2, FINE), bf16), pltpu.VMEM((8, 2, FINE), bf16),
            pltpu.SemaphoreType.DMA((3,)),
        ],
        far=(0, 1, 2),
    )
    low, high = from_below(upper), from_above(lower)
    pieces = jnp.transpose(up_weight.reshape(27, 16, 8, 16), (1, 3, 0, 2)).reshape(16, 16, 216)
    mixed, pair, cot_planes = call(
        mix_kernel,
        [((16, 16, 640), bf16), ((2, 16, COARSE), bf16), ((32, SLAB), bf16)],
        (pieces, here, low, high, own_cot),
    )
    mixed, second_own, up_shared = lax.optimization_barrier((mixed, second_own, up_first))
    kernels = lax.all_gather(jnp.concatenate([second_own, up_shared], axis=1), "ch", axis=0)
    cot_planes = lax.all_gather(cot_planes, "ch", axis=0)

    partial, joined = call(
        up_kernel,
        [((16, 16, FINE + 128), bf16), ((16, HALOED), bf16)],
        (swap(mixed, "ch"), own_skip, low, high, up_first, skip_first),
        [pltpu.VMEM((144, HALOED), bf16)],
        near_outs=(1,),
    )
    pre, stats = call(
        first_sum_kernel,
        [((8, SLAB), f32), ((slabs, 16, FINE // 2 + 128), bf16)],
        (swap(partial, "ch"),),
    )
    (packed,) = call(
        first_norm_kernel, [((16, 16, SLAB + 128), bf16)], (pre, swap(stats, "gz"))
    )
    packed, kernels = lax.optimization_barrier((packed, kernels))
    packed = swap(packed, "ch")
    forward, backward, first = call(
        matrix_kernel,
        [((128, 3456), bf16), ((128, 3456), bf16), ((144, 3456), bf16)],
        (kernels, skip_first),
        [pltpu.VMEM((128, 3456), bf16), pltpu.VMEM((144, 3456), bf16), pltpu.SemaphoreType.DMA((2,))],
        far_outs=(1, 2),
        near_outs=(0,),
    )
    unfolded = pltpu.VMEM((9, 128, HALOED), bf16)
    second_pre, low, high, stats = call(
        second_conv_kernel,
        [
            ((128, SLAB), f32), ((128, FINE), bf16), ((128, FINE), bf16), ((slabs, 2, 128), f32),
        ],
        (packed, forward),
        [unfolded],
        14,
        near=(1,),
        near_outs=(0, 1, 2),
    )
    decoded, normed, slope, inverse, sums = call(
        second_norm_kernel,
        [
            ((8, SLAB), bf16), ((128, HALOED), f32), ((128, HALOED), f32), ((8, 128), f32),
            ((slabs, 2, 128), f32),
        ],
        (second_pre, from_below(high), from_above(low), swap(stats, "gz"), cot_planes),
        [pltpu.VMEM((16, 16, SLAB), bf16), pltpu.SemaphoreType.DMA((1,))],
        far=(4,),
        near=(0,),
        near_outs=(1, 2),
    )
    low, high, slope_one, sums, second_grad = call(
        second_back_kernel,
        [
            ((128, FINE), bf16), ((128, FINE), bf16), ((128, SLAB), f32), ((slabs, 2, 128), f32),
            ((216, 128), f32),
        ],
        (
            normed, slope, inverse, swap(sums, "gz"), packed, backward,
        ),
        [
            unfolded, pltpu.VMEM((128, SLAB), f32), pltpu.VMEM((3, 128, 128), f32),
            pltpu.VMEM((128, 3456), bf16), pltpu.VMEM((144, HALOED), bf16), pltpu.SemaphoreType.DMA((1,)),
        ],
        15,
        far=(5,),
        near=(0, 1),
        near_outs=(0, 1, 2, 4),
    )
    skip_grad, coarse_own, coarse_next, weight_grads = call(
        first_back_kernel,
        [((8, SLAB), bf16), ((16, COARSE), f32), ((16, COARSE), f32), ((GRAD_ROWS, 128), bf16)],
        (
            slope_one, from_below(high), from_above(low), swap(sums, "gz"), packed, first,
            up_own, pair, joined, second_grad,
        ),
        [
            unfolded, pltpu.VMEM((128, SLAB), f32), pltpu.VMEM((3, 128, 128), f32),
            pltpu.VMEM((1152, 2 * COARSE), bf16), pltpu.VMEM((16, 3456), bf16),
            pltpu.VMEM((144, 3456), bf16), pltpu.VMEM((144, HALOED), bf16), pltpu.SemaphoreType.DMA((1,)),
        ],
        17,
        far=(5,),
        near=(0, 8, 9),
    )
    coarse_grad = (coarse_own + from_below(coarse_next)).astype(bf16)
    rows = GRAD_ROWS // slabs
    (spread,) = call(
        grad_sum_kernel,
        [((slabs, rows, 128), bf16)],
        (swap(weight_grads.reshape(slabs, rows, 128), "gz"),),
    )
    grads = call(
        grad_split_kernel,
        [((27, 16, 128), f32), ((27, 8, 128), f32), ((27, 8, 128), f32), ((27, 8, 128), f32)],
        (swap(spread, "gz"),),
    )
    grads = [jnp.transpose(grad, (0, 2, 1)) for grad in grads]
    return (
        decoded.reshape(8, 2, FINE),
        coarse_grad.reshape(16, 1, COARSE),
        skip_grad.reshape(8, 2, FINE),
        *grads,
    )


def solution(mesh):
    volume, kernel = P("ch", "gz", None), P(None, None, "ch")
    return jax.shard_map(
        local,
        mesh=mesh,
        in_specs=(volume, volume, kernel, kernel, kernel, kernel, volume),
        out_specs=(volume, volume, volume, kernel, kernel, kernel, kernel),
        check_vma=False,
    )
```

```python
import math

import jax
import jax.numpy as jnp
from jax import lax
from jax.experimental import pallas as pl
from jax.experimental.pallas import tpu as pltpu
from jax.sharding import PartitionSpec as P

C_OUT = 128
XC = 16
YC = 8
COARSE = YC * XC
FINE = 4 * COARSE
SLAB = 2 * FINE
HALOED = 4 * FINE
WIDE = 6 * FINE
LEAK_SLOPE = 0.01
KINK_WIDTH = 0.01
NORM_EPS = 1e-05
PARITY = (((1, 0),), ((2, 0), (0, 1)))
GRAD_ROWS = 1280

f32 = jnp.float32
bf16 = jnp.bfloat16


def activate(u):
    q = u * u + KINK_WIDTH
    return 0.5 * (1.0 + LEAK_SLOPE) * u + 0.5 * (1.0 - LEAK_SLOPE) * (q * lax.rsqrt(q))


def activate_slope(u):
    return 0.5 * (1.0 + LEAK_SLOPE) + 0.5 * (1.0 - LEAK_SLOPE) * (
        u * lax.rsqrt(u * u + KINK_WIDTH)
    )


def shift(values, step_y, step_x, rows, columns):
    if step_y == 0 and step_x == 0:
        return values
    extent = values.shape[-1]
    cell = lax.broadcasted_iota(jnp.int32, (1, extent), 1)
    column = cell % columns + step_x
    row = cell // columns % rows + step_y
    inside = (column >= 0) & (column < columns) & (row >= 0) & (row < rows)
    moved = pltpu.roll(values, (-(step_y * columns + step_x)) % extent, 1)
    return moved * jnp.where(inside, 1.0, 0.0)


def fine_shift(values, step_y, step_x):
    return shift(values, step_y, step_x, 2 * YC, 2 * XC)


def coarse_shift(values, step_y, step_x):
    return shift(values, step_y, step_x, YC, XC)


def interleave_matrix(transposed):
    fine_dim = 0 if transposed else 1
    cell = lax.broadcasted_iota(jnp.int32, (FINE, FINE), fine_dim)
    other = lax.broadcasted_iota(jnp.int32, (FINE, FINE), 1 - fine_dim)
    y, x = cell // (2 * XC), cell % (2 * XC)
    source = ((y % 2) * 2 + x % 2) * COARSE + (y // 2) * XC + x // 2
    return jnp.where(source == other, 1.0, 0.0).astype(bf16)


def edge_mask(slab, slabs, width):
    plane = lax.broadcasted_iota(jnp.int32, (1, SLAB + 2 * width * FINE), 1) // FINE
    outside = ((plane < width) & (slab == 0)) | ((plane > width + 1) & (slab == slabs - 1))
    return jnp.where(outside, 0.0, 1.0)


def as_row(column):
    return jnp.transpose(jnp.broadcast_to(column, (C_OUT, C_OUT)))[:1]


def as_column(row):
    return jnp.transpose(jnp.broadcast_to(row, (C_OUT, C_OUT)))[:, :1]


def call(kernel, outs, args, scratch=(), megabytes=8, far=(), far_outs=(), near=(), near_outs=()):
    args = list(args)
    for index in far:
        args[index] = pltpu.with_memory_space_constraint(args[index], pltpu.HBM)
    for index in near:
        args[index] = pltpu.with_memory_space_constraint(args[index], pltpu.VMEM)

    def spec(index, which):
        return pl.BlockSpec(memory_space=pltpu.HBM if index in which else pltpu.VMEM)

    def out(index, shape, dtype):
        if index in far_outs:
            return pltpu.HBM(shape, dtype)
        return pltpu.VMEM(shape, dtype) if index in near_outs else jax.ShapeDtypeStruct(shape, dtype)

    return pl.pallas_call(
        kernel,
        out_shape=[out(index, *shape) for index, shape in enumerate(outs)],
        in_specs=[spec(index, far) for index in range(len(args))],
        out_specs=[spec(index, far_outs) for index in range(len(outs))],
        scratch_shapes=list(scratch),
        compiler_params=pltpu.CompilerParams(vmem_limit_bytes=megabytes * 2**20),
    )(*args)


def copies(sources, targets, semaphores):
    started = []
    for index, (source, target) in enumerate(zip(sources, targets)):
        copy = pltpu.make_async_copy(source, target, semaphores.at[index])
        copy.start()
        started.append(copy)
    return started


def halo_kernel(
    far_coarse, far_skip, far_cot, upward, downward, own_skip, own_cot, coarse, skip, cotangent, semaphores
):
    for copy in copies((far_coarse, far_skip, far_cot), (coarse, skip, cotangent), semaphores):
        copy.wait()
    cells = coarse[...].astype(f32)
    cells = [cells[:8], cells[8:]]
    skip_planes, cot_planes = skip[...].astype(f32), cotangent[...].astype(f32)
    both = [cot_planes[:, 0], cot_planes[:, 1]]
    upward[...] = jnp.concatenate(cells + [skip_planes[:, 1]] + both, axis=1).astype(bf16)
    downward[...] = jnp.concatenate(cells + [skip_planes[:, 0]] + both, axis=1).astype(bf16)
    own_skip[...] = jnp.concatenate([skip_planes[:, 0], skip_planes[:, 1]], axis=1).astype(bf16)
    own_cot[...] = jnp.concatenate(both, axis=1).astype(bf16)


def mix_kernel(pieces, coarse, low, high, own_cot, mixed, pair, cot_planes):
    below, above = low[...].astype(f32), high[...].astype(f32)
    here = coarse[...].astype(f32)
    before = jnp.concatenate([below[:, :COARSE], below[:, COARSE : 2 * COARSE]], axis=0)
    after = jnp.concatenate([above[:, :COARSE], above[:, COARSE : 2 * COARSE]], axis=0)
    planes = jnp.concatenate([before, here, after], axis=1).astype(bf16)
    mixed[:, :, :256] = jnp.zeros((16, 16, 256), bf16)
    for target in range(16):
        mixed[target, :, :216] = pieces[target]
        mixed[target, :, 256:] = planes
    pair[0] = coarse[...]
    pair[1] = after.astype(bf16)
    cot = own_cot[...].astype(f32)
    at = 2 * COARSE + FINE
    slabs = [below[:, at:], cot, above[:, at:], jnp.zeros((8, SLAB), f32)]
    cot_planes[...] = jnp.concatenate(slabs, axis=0).astype(bf16)


def up_kernel(mixed, own_skip, low, high, first_up, first_skip, partial, joined, unfolded):
    slab = lax.axis_index("gz")
    packed = mixed[...]
    weights = packed[:, :, :256].reshape(256, 256)
    mixture = []
    for plane in range(3):
        source = packed[:, :, 256 + plane * COARSE : 256 + (plane + 1) * COARSE].reshape(256, COARSE)
        mixture.append(
            lax.dot_general(weights, source, (((0,), (0,)), ((), ())), preferred_element_type=f32)
        )
    rows = []
    for sources in (((2, 0), (0, 1)), ((1, 1),), ((2, 1), (0, 2)), ((1, 2),)):
        cells = []
        for y_par in (0, 1):
            for x_par in (0, 1):
                total = None
                for k_z, plane in sources:
                    for k_y, y_off in PARITY[y_par]:
                        for k_x, x_off in PARITY[x_par]:
                            tap = k_z * 9 + k_y * 3 + k_x
                            term = coarse_shift(mixture[plane][tap * 8 : tap * 8 + 8], y_off, x_off)
                            total = term if total is None else total + term
                cells.append(total)
        rows.append(jnp.concatenate(cells, axis=1))
    spread = jnp.concatenate(rows, axis=0).astype(bf16)
    fine = jnp.dot(spread, interleave_matrix(False), preferred_element_type=f32)
    first_inside = jnp.where(slab == 0, 0.0, 1.0)
    upsampled = jnp.concatenate(
        [fine[0:8] * first_inside, fine[8:16], fine[16:24], fine[24:32]], axis=1
    )
    skip_at = slice(2 * COARSE, 2 * COARSE + FINE)
    skip = jnp.concatenate(
        [low[:, skip_at].astype(f32), own_skip[...].astype(f32), high[:, skip_at].astype(f32)], axis=1
    )
    features = jnp.concatenate([upsampled, skip], axis=0)
    joined[...] = features.astype(bf16)
    for tap in range(9):
        unfolded[tap * 16 : tap * 16 + 16, :] = fine_shift(features, tap // 3 - 1, tap % 3 - 1).astype(bf16)
    total = jnp.zeros((C_OUT, SLAB), f32)
    for k_z in range(3):
        matrix = []
        for tap in range(9):
            up_part = first_up[k_z * 9 + tap].astype(f32)
            skip_part = first_skip[k_z * 9 + tap].astype(f32)
            matrix.append(jnp.concatenate([up_part, skip_part], axis=0))
        matrix = jnp.concatenate(matrix, axis=0).astype(bf16)
        total = total + lax.dot_general(
            matrix,
            unfolded[:, k_z * FINE : k_z * FINE + SLAB],
            (((0,), (0,)), ((), ())),
            preferred_element_type=f32,
        )
    mean = jnp.sum(total, axis=1, keepdims=True) / SLAB
    deviation = total - mean
    first = jnp.concatenate([deviation[:, :FINE], in_parts(mean)], axis=1).reshape(16, 8, FINE + 128)
    second = jnp.concatenate([deviation[:, FINE:], jnp.zeros((C_OUT, 128), f32)], axis=1)
    partial[...] = jnp.concatenate([first, second.reshape(16, 8, FINE + 128)], axis=1).astype(bf16)


def in_parts(values):
    high = values.astype(bf16).astype(f32)
    middle = (values - high).astype(bf16).astype(f32)
    rest = values - high - middle
    lane = lax.broadcasted_iota(jnp.int32, (values.shape[0], 128), 1)
    return jnp.where(
        lane == 0, high, jnp.where(lane == 1, middle, jnp.where(lane == 2, rest, 0.0))
    )


def first_sum_kernel(parts, pre, stats):
    slab = lax.axis_index("gz")
    both = jnp.sum(parts[...].astype(f32), axis=0)
    total = jnp.concatenate([both[:8, :FINE], both[8:, :FINE]], axis=1)
    total = total + jnp.sum(both[:8, FINE:], axis=1, keepdims=True)
    pre[...] = total
    mean = jnp.sum(total, axis=1, keepdims=True) / SLAB
    deviation = total - mean
    square = jnp.sum(deviation * deviation, axis=1, keepdims=True)
    tail = in_parts(jnp.concatenate([mean, square], axis=0))
    half = FINE // 2
    first = jnp.concatenate([deviation[:, :half], deviation[:, half:FINE]], axis=0)
    last = jnp.concatenate([deviation[:, FINE : FINE + half], deviation[:, FINE + half :]], axis=0)
    first = jnp.concatenate([first, tail], axis=1).astype(bf16)
    last = jnp.concatenate([last, tail], axis=1).astype(bf16)
    for target in range(stats.shape[0]):
        above = target > slab

        @pl.when(above)
        def _():
            stats[target] = last

        @pl.when(jnp.logical_not(above))
        def _():
            stats[target] = first


def first_norm_kernel(pre, stats, packed):
    slab, slabs = lax.axis_index("gz"), stats.shape[0]
    half = FINE // 2
    tails = jnp.sum(stats[:, :, half:].astype(f32), axis=2, keepdims=True)
    means = tails[:, :8]
    mean = jnp.sum(means, axis=0) / slabs
    apart = means - mean[None]
    square = jnp.sum(tails[:, 8:] + SLAB * apart * apart, axis=0)
    inverse = lax.rsqrt(square / (slabs * SLAB) + NORM_EPS)

    def neighbour(index):
        block = stats[index].astype(f32)
        centre = jnp.sum(block[:8, half:], axis=1, keepdims=True)
        return jnp.concatenate([block[:8, :half], block[8:, :half]], axis=1) + centre

    low, high = neighbour(jnp.maximum(slab - 1, 0)), neighbour(jnp.minimum(slab + 1, slabs - 1))
    lower = jnp.concatenate([low, pre[:, :FINE]], axis=1)
    upper = jnp.concatenate([pre[:, FINE:], high], axis=1)
    wide = jnp.broadcast_to(inverse, (8, 128))
    main = wide.astype(bf16).astype(f32)
    block = jnp.concatenate(
        [
            jnp.concatenate([(lower - mean) * inverse, main], axis=1),
            jnp.concatenate([(upper - mean) * inverse, wide - main], axis=1),
        ],
        axis=0,
    ).astype(bf16)
    for target in range(16):
        packed[target] = block


def read_planes(packed, block):
    pair = packed[pl.ds(2 * block, 2), 0:16, :SLAB].astype(f32)
    return jnp.concatenate([pair[:, :8].reshape(16, SLAB), pair[:, 8:].reshape(16, SLAB)], axis=1)


def unfold_block(values, unfolded, block, sign):
    for tap in range(9):
        moved = fine_shift(values, sign * (tap // 3 - 1), sign * (tap % 3 - 1))
        unfolded[tap, pl.ds(pl.multiple_of(block * 16, 16), 16), :] = moved.astype(bf16)


def tap_matrix(weights, tap, first):
    both = weights[:, tap].astype(f32)
    return both[:, first * 8 : first * 8 + 8].reshape(C_OUT, C_OUT)


def matrix_kernel(weights, first_skip, forward, far_backward, far_first, backward, first, semaphores):
    for tap in range(27):
        at = slice(tap * 128, tap * 128 + 128)
        second = tap_matrix(weights, tap, 0)
        forward[:, at] = jnp.transpose(second).astype(bf16)
        backward[:, at] = second.astype(bf16)
        skip_part = jnp.concatenate([first_skip[tap].astype(f32), jnp.zeros((8, 128), f32)], axis=0)
        first[0:128, at] = tap_matrix(weights, tap, 1).astype(bf16)
        first[128:144, at] = skip_part.astype(bf16)
    for copy in copies((backward, first), (far_backward, far_first), semaphores):
        copy.wait()


def second_conv_kernel(
    packed, matrix, pre, halo, stats, unfolded
):
    mask = edge_mask(lax.axis_index("gz"), stats.shape[0], 1)

    def prepare(block, carry):
        hidden = activate(read_planes(packed, block)).astype(bf16).astype(f32) * mask
        unfold_block(hidden, unfolded, block, 1)
        return carry

    lax.fori_loop(0, 8, prepare, 0)
    total = jnp.zeros((C_OUT, SLAB), f32)
    for k_z in range(3):
        total = total + jnp.dot(
            matrix[:, k_z * 1152 : k_z * 1152 + 1152],
            unfolded[:, :, k_z * FINE : k_z * FINE + SLAB].reshape(1152, SLAB),
            preferred_element_type=f32,
        )
    pre[...] = total
    mean = jnp.sum(total, axis=1, keepdims=True) / SLAB
    deviation = total - mean
    square = jnp.sum(deviation * deviation, axis=1, keepdims=True)
    halo[...] = deviation.astype(bf16)
    row = lax.broadcasted_iota(jnp.int32, (2, 128), 0)
    tile = jnp.where(row < 1, as_row(mean), as_row(square))
    stats[...] = jnp.broadcast_to(tile[None], stats.shape)


def second_norm_kernel(
    pre, low, high, stats, far_cot, decoded, normed, slope, inverse_out, sums, cotangent, semaphores
):
    (fetch,) = copies((far_cot,), (cotangent,), semaphores)
    slab, share = lax.axis_index("gz"), lax.axis_index("ch")
    slabs = stats.shape[0]
    gathered = stats[...]
    means = gathered[:, 0:1]
    mean_row = jnp.sum(means, axis=0) / slabs
    apart = means - mean_row[None]
    square = jnp.sum(gathered[:, 1:2] + SLAB * apart * apart, axis=0)
    inverse_row = lax.rsqrt(square / (slabs * SLAB) + NORM_EPS)
    inverse_out[...] = jnp.broadcast_to(inverse_row, inverse_out.shape)
    below = stats[jnp.maximum(slab - 1, 0)][0:1] - mean_row
    above = stats[jnp.minimum(slab + 1, slabs - 1)][0:1] - mean_row
    mean, inverse = as_column(mean_row), as_column(inverse_row)
    normed[:, :SLAB] = (low[...].astype(f32) + as_column(below)) * inverse
    normed[:, SLAB : 2 * SLAB] = (pre[...] - mean) * inverse
    normed[:, 2 * SLAB :] = (high[...].astype(f32) + as_column(above)) * inverse
    own = normed[pl.ds(pl.multiple_of(share * 8, 8), 8), SLAB : 2 * SLAB]
    decoded[...] = activate(own).astype(bf16)

    def prepare(block, carry):
        at = pl.ds(pl.multiple_of(block * 16, 16), 16)
        pair = cotangent[pl.ds(2 * block, 2)].astype(f32)
        planes = [pair[:, row : row + 8].reshape(16, SLAB) for row in (0, 8, 16)]
        slope[at, :] = jnp.concatenate(planes, axis=1) * activate_slope(normed[at, :])
        return carry

    fetch.wait()
    lax.fori_loop(0, 8, prepare, 0)
    inner = slope[:, SLAB : 2 * SLAB]
    one = as_row(jnp.sum(inner, axis=1, keepdims=True))
    two = as_row(jnp.sum(inner * normed[:, SLAB : 2 * SLAB], axis=1, keepdims=True))
    row = lax.broadcasted_iota(jnp.int32, (2, 128), 0)
    sums[...] = jnp.broadcast_to(jnp.where(row < 1, one, two)[None], sums.shape)


def total_means(sums):
    totals = jnp.sum(sums[...], axis=0) / (sums.shape[0] * SLAB)
    return as_column(totals[0:1]), as_column(totals[1:2])


def second_back_kernel(
    normed, slope, inverse_row, sums_in, packed, far_matrix,
    slope_one, sums, weight_grad,
    unfolded, grads, columns, matrix, own_unfolded, semaphores,
):
    (fetch,) = copies((far_matrix,), (matrix,), semaphores)
    slab, share = lax.axis_index("gz"), lax.axis_index("ch")
    mask = edge_mask(slab, sums.shape[0], 2)
    mean_grad, mean_cross = total_means(sums_in)
    columns[0] = jnp.broadcast_to(mean_grad, (C_OUT, 128))
    columns[1] = jnp.broadcast_to(mean_cross, (C_OUT, 128))
    columns[2] = jnp.broadcast_to(as_column(inverse_row[0:1]), (C_OUT, 128))

    def prepare(block, carry):
        at = pl.ds(pl.multiple_of(block * 16, 16), 16)
        grad = columns[2, at, :1] * (slope[at, :] - columns[0, at, :1] - normed[at, :] * columns[1, at, :1])
        grad = grad.astype(bf16).astype(f32) * mask
        grads[at, :] = grad[:, SLAB : 2 * SLAB]
        unfold_block(grad, unfolded, block, -1)
        return carry

    lax.fori_loop(0, 8, prepare, 0)
    fetch.wait()
    total = jnp.zeros((C_OUT, HALOED), f32)
    for k_z in range(3):
        total = total + jnp.dot(
            matrix[:, k_z * 1152 : k_z * 1152 + 1152],
            unfolded[:, :, (2 - k_z) * FINE : (2 - k_z) * FINE + HALOED].reshape(1152, HALOED),
            preferred_element_type=f32,
        )
    both = packed[:, :, :SLAB].astype(f32)
    first_normed = jnp.concatenate(
        [both[:, :8].reshape(C_OUT, SLAB), both[:, 8:].reshape(C_OUT, SLAB)], axis=1
    )
    whole = total * activate_slope(first_normed)
    slope_one[...] = whole
    inner = whole[:, FINE : 3 * FINE]
    one = as_row(jnp.sum(inner, axis=1, keepdims=True))
    two = as_row(jnp.sum(inner * first_normed[:, FINE : 3 * FINE], axis=1, keepdims=True))
    row = lax.broadcasted_iota(jnp.int32, (2, 128), 0)
    sums[...] = jnp.broadcast_to(jnp.where(row < 1, one, two)[None], sums.shape)
    own = activate(read_planes(packed, share // 2)).astype(bf16).astype(f32)
    own = own * edge_mask(slab, sums.shape[0], 1)
    for tap in range(9):
        own_unfolded[tap * 16 : tap * 16 + 16, :] = fine_shift(own, tap // 3 - 1, tap % 3 - 1).astype(bf16)
    odd = share % 2 == 1
    turned = jnp.transpose(grads[...]).astype(bf16)
    for k_z in range(3):
        product = jnp.dot(
            own_unfolded[:, k_z * FINE : k_z * FINE + SLAB], turned, preferred_element_type=f32
        ).reshape(9, 2, 8, 128)
        weight_grad[k_z * 72 : k_z * 72 + 72, :] = jnp.where(odd, product[:, 1], product[:, 0]).reshape(72, 128)


def first_back_kernel(
    slope, sums_in, packed, far_matrix, up_weight, coarse, joined, second_grad,
    skip_grad, coarse_own, coarse_next, weight_grads,
    unfolded, grads, columns, spread, up_matrix, matrix, own_unfolded, semaphores,
):
    (fetch,) = copies((far_matrix,), (matrix,), semaphores)
    slab = lax.axis_index("gz")
    mask = edge_mask(slab, sums_in.shape[0], 1)
    mean_grad, mean_cross = total_means(sums_in)
    columns[0] = jnp.broadcast_to(mean_grad, (C_OUT, 128))
    columns[1] = jnp.broadcast_to(mean_cross, (C_OUT, 128))
    wide = packed[:, :, SLAB:].astype(f32)
    columns[2] = (wide[:, :8] + wide[:, 8:]).reshape(C_OUT, 128)

    def prepare(block, carry):
        at = pl.ds(pl.multiple_of(block * 16, 16), 16)
        normed = read_planes(packed, block)
        grad = columns[2, at, :1] * (slope[at, :] - columns[0, at, :1] - normed * columns[1, at, :1])
        grad = grad.astype(bf16).astype(f32) * mask
        grads[at, :] = grad[:, FINE : 3 * FINE]
        unfold_block(grad, unfolded, block, -1)
        return carry

    lax.fori_loop(0, 8, prepare, 0)
    fetch.wait()
    total = jnp.zeros((144, SLAB), f32)
    for k_z in range(3):
        total = total + jnp.dot(
            matrix[:, k_z * 1152 : k_z * 1152 + 1152],
            unfolded[:, :, (2 - k_z) * FINE : (2 - k_z) * FINE + SLAB].reshape(1152, SLAB),
            preferred_element_type=f32,
        )
    skip_grad[...] = total[128:136].astype(bf16)
    d_up = jnp.concatenate([total[:128, :FINE], total[:128, FINE:]], axis=0).astype(bf16)
    last = (((1,), (1,)), ((), ()))
    parted = jnp.dot(d_up, interleave_matrix(True), preferred_element_type=f32)
    for y_par in (0, 1):
        for x_par in (0, 1):
            at = (y_par * 2 + x_par) * COARSE
            source = jnp.concatenate(
                [parted[:128, at : at + COARSE], parted[128:, at : at + COARSE]], axis=1
            )
            for k_y, y_off in PARITY[y_par]:
                for k_x, x_off in PARITY[x_par]:
                    tap = k_y * 3 + k_x
                    spread[tap * 128 : tap * 128 + 128, :] = coarse_shift(
                        source, -y_off, -x_off
                    ).astype(bf16)
    for tap in range(27):
        at = (tap // 9) * 1152 + (tap % 9) * 128
        up_matrix[:, at : at + 128] = up_weight[tap]
    low_plane, high_plane = spread[:, :COARSE], spread[:, COARSE:]
    coarse_own[...] = jnp.dot(
        up_matrix[:, 1152:2304], low_plane, preferred_element_type=f32
    ) + jnp.dot(up_matrix[:, 2304:], high_plane, preferred_element_type=f32)
    coarse_next[...] = jnp.dot(up_matrix[:, :1152], high_plane, preferred_element_type=f32)
    here, following = coarse[0], coarse[1]
    for k_z, source, plane in ((0, following, high_plane), (1, here, low_plane), (2, here, high_plane)):
        product = lax.dot_general(source, plane, last, preferred_element_type=f32)
        for tap in range(9):
            at = (k_z * 9 + tap) * 16
            weight_grads[at : at + 16, :] = product[:, tap * 128 : tap * 128 + 128].astype(bf16)
    own = joined[...].astype(f32)
    for tap in range(9):
        own_unfolded[tap * 16 : tap * 16 + 16, :] = fine_shift(own, tap // 3 - 1, tap % 3 - 1).astype(bf16)
    turned = jnp.transpose(grads[...]).astype(bf16)
    for k_z in range(3):
        product = jnp.dot(
            own_unfolded[:, k_z * FINE : k_z * FINE + SLAB], turned, preferred_element_type=f32
        )
        weight_grads[432 + k_z * 144 : 576 + k_z * 144, :] = product.astype(bf16)
    rest = jnp.concatenate([second_grad[...], jnp.zeros((GRAD_ROWS - 1080, 128), f32)], axis=0)
    weight_grads[864:, :] = rest.astype(bf16)


def grad_sum_kernel(parts, spread):
    total = jnp.sum(parts[...].astype(f32), axis=0) * (1.0 / math.sqrt(SLAB))
    spread[...] = jnp.broadcast_to(total.astype(bf16)[None], spread.shape)


def grad_split_kernel(gathered, up, first_up, first_skip, second):
    values = gathered[...].reshape(GRAD_ROWS, 128).astype(f32)
    up[...] = values[:432].reshape(27, 16, 128)
    first = values[432:864].reshape(27, 16, 128)
    first_up[...] = first[:, :8]
    first_skip[...] = first[:, 8:]
    second[...] = values[864:1080].reshape(27, 8, 128)


def local(coarse, encoder_skip, up_weight, first_up, first_skip, second_weight, cotangent):
    slabs, shares = lax.axis_size("gz"), lax.axis_size("ch")
    upward = [(i, i + 1) for i in range(slabs - 1)]
    downward = [(i + 1, i) for i in range(slabs - 1)]

    def from_below(block):
        return lax.ppermute(block, "gz", upward)

    def from_above(block):
        return lax.ppermute(block, "gz", downward)

    def swap(block, axis):
        return lax.all_to_all(block, axis, 0, 0, tiled=True)

    def io_major(weight):
        return jnp.transpose(weight, (0, 2, 1))

    up_own, up_first = io_major(up_weight), io_major(first_up)
    skip_first, second_own = io_major(first_skip), io_major(second_weight)

    here = coarse.reshape(16, COARSE)
    halo = ((8, 2 * COARSE + 3 * FINE), bf16)
    upper, lower, own_skip, own_cot = call(
        halo_kernel,
        [halo, halo, ((8, SLAB), bf16), ((8, SLAB), bf16)],
        (here, encoder_skip, cotangent),
        [
            pltpu.VMEM((16, COARSE), bf16), pltpu.VMEM((8, 2, FINE), bf16), pltpu.VMEM((8, 2, FINE), bf16),
            pltpu.SemaphoreType.DMA((3,)),
        ],
        far=(0, 1, 2),
    )
    low, high = from_below(upper), from_above(lower)
    pieces = jnp.transpose(up_weight.reshape(27, 16, 8, 16), (1, 3, 0, 2)).reshape(16, 16, 216)
    mixed, pair, cot_planes = call(
        mix_kernel,
        [((16, 16, 640), bf16), ((2, 16, COARSE), bf16), ((32, SLAB), bf16)],
        (pieces, here, low, high, own_cot),
    )
    mixed, second_own, up_shared = lax.optimization_barrier((mixed, second_own, up_first))
    kernels = lax.all_gather(jnp.concatenate([second_own, up_shared], axis=1), "ch", axis=0)
    cot_planes = lax.all_gather(cot_planes, "ch", axis=0)

    partial, joined = call(
        up_kernel,
        [((16, 16, FINE + 128), bf16), ((16, HALOED), bf16)],
        (swap(mixed, "ch"), own_skip, low, high, up_first, skip_first),
        [pltpu.VMEM((144, HALOED), bf16)],
        near_outs=(1,),
    )
    pre, stats = call(
        first_sum_kernel,
        [((8, SLAB), f32), ((slabs, 16, FINE // 2 + 128), bf16)],
        (swap(partial, "ch"),),
    )
    (packed,) = call(
        first_norm_kernel, [((16, 16, SLAB + 128), bf16)], (pre, swap(stats, "gz"))
    )
    packed, kernels = lax.optimization_barrier((packed, kernels))
    packed = swap(packed, "ch")
    forward, backward, first = call(
        matrix_kernel,
        [((128, 3456), bf16), ((128, 3456), bf16), ((144, 3456), bf16)],
        (kernels, skip_first),
        [pltpu.VMEM((128, 3456), bf16), pltpu.VMEM((144, 3456), bf16), pltpu.SemaphoreType.DMA((2,))],
        far_outs=(1, 2),
        near_outs=(0,),
    )
    unfolded = pltpu.VMEM((9, 128, HALOED), bf16)
    second_pre, halo, stats = call(
        second_conv_kernel,
        [
            ((128, SLAB), f32), ((128, SLAB), bf16), ((slabs, 2, 128), f32),
        ],
        (packed, forward),
        [unfolded],
        14,
        near=(1,),
        near_outs=(0, 1),
    )
    decoded, normed, slope, inverse, sums = call(
        second_norm_kernel,
        [
            ((8, SLAB), bf16), ((128, WIDE), f32), ((128, WIDE), f32), ((8, 128), f32),
            ((slabs, 2, 128), f32),
        ],
        (second_pre, from_below(halo), from_above(halo), swap(stats, "gz"), cot_planes),
        [pltpu.VMEM((16, 32, SLAB), bf16), pltpu.SemaphoreType.DMA((1,))],
        far=(4,),
        near=(0,),
        near_outs=(1, 2),
    )
    slope_one, sums, second_grad = call(
        second_back_kernel,
        [
            ((128, HALOED), f32), ((slabs, 2, 128), f32), ((216, 128), f32),
        ],
        (
            normed, slope, inverse, swap(sums, "gz"), packed, backward,
        ),
        [
            pltpu.VMEM((9, 128, WIDE), bf16), pltpu.VMEM((128, SLAB), f32), pltpu.VMEM((3, 128, 128), f32),
            pltpu.VMEM((128, 3456), bf16), pltpu.VMEM((144, HALOED), bf16), pltpu.SemaphoreType.DMA((1,)),
        ],
        20,
        far=(5,),
        near=(0, 1),
        near_outs=(0, 2),
    )
    skip_grad, coarse_own, coarse_next, weight_grads = call(
        first_back_kernel,
        [((8, SLAB), bf16), ((16, COARSE), f32), ((16, COARSE), f32), ((GRAD_ROWS, 128), bf16)],
        (
            slope_one, swap(sums, "gz"), packed, first,
            up_own, pair, joined, second_grad,
        ),
        [
            unfolded, pltpu.VMEM((128, SLAB), f32), pltpu.VMEM((3, 128, 128), f32),
            pltpu.VMEM((1152, 2 * COARSE), bf16), pltpu.VMEM((16, 3456), bf16),
            pltpu.VMEM((144, 3456), bf16), pltpu.VMEM((144, HALOED), bf16), pltpu.SemaphoreType.DMA((1,)),
        ],
        17,
        far=(3,),
        near=(0, 6, 7),
    )
    coarse_grad = (coarse_own + from_below(coarse_next)).astype(bf16)
    rows = GRAD_ROWS // slabs
    (spread,) = call(
        grad_sum_kernel,
        [((slabs, rows, 128), bf16)],
        (swap(weight_grads.reshape(slabs, rows, 128), "gz"),),
    )
    grads = call(
        grad_split_kernel,
        [((27, 16, 128), f32), ((27, 8, 128), f32), ((27, 8, 128), f32), ((27, 8, 128), f32)],
        (swap(spread, "gz"),),
    )
    grads = [jnp.transpose(grad, (0, 2, 1)) for grad in grads]
    return (
        decoded.reshape(8, 2, FINE),
        coarse_grad.reshape(16, 1, COARSE),
        skip_grad.reshape(8, 2, FINE),
        *grads,
    )


def solution(mesh):
    volume, kernel = P("ch", "gz", None), P(None, None, "ch")
    return jax.shard_map(
        local,
        mesh=mesh,
        in_specs=(volume, volume, kernel, kernel, kernel, kernel, volume),
        out_specs=(volume, volume, volume, kernel, kernel, kernel, kernel),
        check_vma=False,
    )
```

```python
import math

import jax
import jax.numpy as jnp
from jax import lax
from jax.experimental import pallas as pl
from jax.experimental.pallas import tpu as pltpu
from jax.sharding import PartitionSpec as P

C_OUT = 128
XC = 16
YC = 8
COARSE = YC * XC
FINE = 4 * COARSE
SLAB = 2 * FINE
HALOED = 4 * FINE
WIDE = 6 * FINE
LEAK_SLOPE = 0.01
KINK_WIDTH = 0.01
NORM_EPS = 1e-05
PARITY = (((1, 0),), ((2, 0), (0, 1)))
GRAD_ROWS = 1280

f32 = jnp.float32
bf16 = jnp.bfloat16


def activate(u):
    q = u * u + KINK_WIDTH
    return 0.5 * (1.0 + LEAK_SLOPE) * u + 0.5 * (1.0 - LEAK_SLOPE) * (q * lax.rsqrt(q))


def activate_slope(u):
    return 0.5 * (1.0 + LEAK_SLOPE) + 0.5 * (1.0 - LEAK_SLOPE) * (
        u * lax.rsqrt(u * u + KINK_WIDTH)
    )


def shift(values, step_y, step_x, rows, columns):
    if step_y == 0 and step_x == 0:
        return values
    extent = values.shape[-1]
    cell = lax.broadcasted_iota(jnp.int32, (1, extent), 1)
    column = cell % columns + step_x
    row = cell // columns % rows + step_y
    inside = (column >= 0) & (column < columns) & (row >= 0) & (row < rows)
    moved = pltpu.roll(values, (-(step_y * columns + step_x)) % extent, 1)
    return moved * jnp.where(inside, 1.0, 0.0)


def coarse_shift(values, step_y, step_x):
    return shift(values, step_y, step_x, YC, XC)


def interleave_matrix(transposed):
    fine_dim = 0 if transposed else 1
    cell = lax.broadcasted_iota(jnp.int32, (FINE, FINE), fine_dim)
    other = lax.broadcasted_iota(jnp.int32, (FINE, FINE), 1 - fine_dim)
    y, x = cell // (2 * XC), cell % (2 * XC)
    source = ((y % 2) * 2 + x % 2) * COARSE + (y // 2) * XC + x // 2
    return jnp.where(source == other, 1.0, 0.0).astype(bf16)


def edge_mask(slab, slabs, width):
    plane = lax.broadcasted_iota(jnp.int32, (1, SLAB + 2 * width * FINE), 1) // FINE
    outside = ((plane < width) & (slab == 0)) | ((plane > width + 1) & (slab == slabs - 1))
    return jnp.where(outside, 0.0, 1.0)


def as_row(column):
    return jnp.transpose(jnp.broadcast_to(column, (C_OUT, C_OUT)))[:1]


def as_column(row):
    return jnp.transpose(jnp.broadcast_to(row, (C_OUT, C_OUT)))[:, :1]


def call(kernel, outs, args, scratch=(), megabytes=8, far=(), far_outs=(), near=(), near_outs=()):
    args = list(args)
    for index in far:
        args[index] = pltpu.with_memory_space_constraint(args[index], pltpu.HBM)
    for index in near:
        args[index] = pltpu.with_memory_space_constraint(args[index], pltpu.VMEM)

    def spec(index, which):
        return pl.BlockSpec(memory_space=pltpu.HBM if index in which else pltpu.VMEM)

    def out(index, shape, dtype):
        if index in far_outs:
            return pltpu.HBM(shape, dtype)
        return pltpu.VMEM(shape, dtype) if index in near_outs else jax.ShapeDtypeStruct(shape, dtype)

    return pl.pallas_call(
        kernel,
        out_shape=[out(index, *shape) for index, shape in enumerate(outs)],
        in_specs=[spec(index, far) for index in range(len(args))],
        out_specs=[spec(index, far_outs) for index in range(len(outs))],
        scratch_shapes=list(scratch),
        compiler_params=pltpu.CompilerParams(vmem_limit_bytes=megabytes * 2**20),
    )(*args)


def copies(sources, targets, semaphores):
    started = []
    for index, (source, target) in enumerate(zip(sources, targets)):
        copy = pltpu.make_async_copy(source, target, semaphores.at[index])
        copy.start()
        started.append(copy)
    return started


def halo_kernel(
    far_coarse, far_skip, far_cot, upward, downward, own_skip, own_cot, coarse, skip, cotangent, semaphores
):
    for copy in copies((far_coarse, far_skip, far_cot), (coarse, skip, cotangent), semaphores):
        copy.wait()
    cells = coarse[...].astype(f32)
    cells = [cells[:8], cells[8:]]
    skip_planes, cot_planes = skip[...].astype(f32), cotangent[...].astype(f32)
    both = [cot_planes[:, 0], cot_planes[:, 1]]
    upward[...] = jnp.concatenate(cells + [skip_planes[:, 1]] + both, axis=1).astype(bf16)
    downward[...] = jnp.concatenate(cells + [skip_planes[:, 0]] + both, axis=1).astype(bf16)
    own_skip[...] = jnp.concatenate([skip_planes[:, 0], skip_planes[:, 1]], axis=1).astype(bf16)
    own_cot[...] = jnp.concatenate(both, axis=1).astype(bf16)


def mix_kernel(pieces, coarse, low, high, own_cot, mixed, pair, cot_planes):
    below, above = low[...].astype(f32), high[...].astype(f32)
    here = coarse[...].astype(f32)
    before = jnp.concatenate([below[:, :COARSE], below[:, COARSE : 2 * COARSE]], axis=0)
    after = jnp.concatenate([above[:, :COARSE], above[:, COARSE : 2 * COARSE]], axis=0)
    planes = jnp.concatenate([before, here, after], axis=1).astype(bf16)
    mixed[:, :, :256] = jnp.zeros((16, 16, 256), bf16)
    for target in range(16):
        mixed[target, :, :216] = pieces[target]
        mixed[target, :, 256:] = planes
    pair[0] = coarse[...]
    pair[1] = after.astype(bf16)
    cot = own_cot[...].astype(f32)
    at = 2 * COARSE + FINE
    slabs = [below[:, at:], cot, above[:, at:], jnp.zeros((8, SLAB), f32)]
    cot_planes[...] = jnp.concatenate(slabs, axis=0).astype(bf16)


def up_kernel(mixed, own_skip, low, high, first_up, first_skip, partial, joined, unfolded):
    slab = lax.axis_index("gz")
    packed = mixed[...]
    weights = packed[:, :, :256].reshape(256, 256)
    mixture = []
    for plane in range(3):
        source = packed[:, :, 256 + plane * COARSE : 256 + (plane + 1) * COARSE].reshape(256, COARSE)
        mixture.append(
            lax.dot_general(weights, source, (((0,), (0,)), ((), ())), preferred_element_type=f32)
        )
    rows = []
    for sources in (((2, 0), (0, 1)), ((1, 1),), ((2, 1), (0, 2)), ((1, 2),)):
        cells = []
        for y_par in (0, 1):
            for x_par in (0, 1):
                total = None
                for k_z, plane in sources:
                    for k_y, y_off in PARITY[y_par]:
                        for k_x, x_off in PARITY[x_par]:
                            tap = k_z * 9 + k_y * 3 + k_x
                            term = coarse_shift(mixture[plane][tap * 8 : tap * 8 + 8], y_off, x_off)
                            total = term if total is None else total + term
                cells.append(total)
        rows.append(jnp.concatenate(cells, axis=1))
    spread = jnp.concatenate(rows, axis=0).astype(bf16)
    fine = jnp.dot(spread, interleave_matrix(False), preferred_element_type=f32)
    first_inside = jnp.where(slab == 0, 0.0, 1.0)
    upsampled = jnp.concatenate(
        [fine[0:8] * first_inside, fine[8:16], fine[16:24], fine[24:32]], axis=1
    )
    skip_at = slice(2 * COARSE, 2 * COARSE + FINE)
    skip = jnp.concatenate(
        [low[:, skip_at].astype(f32), own_skip[...].astype(f32), high[:, skip_at].astype(f32)], axis=1
    )
    features = jnp.concatenate([upsampled, skip], axis=0)
    joined[...] = features.astype(bf16)
    for tap, moved in enumerate(nine_shifts(features, source_masks(HALOED))):
        unfolded[tap * 16 : tap * 16 + 16, :] = moved.astype(bf16)
    total = jnp.zeros((C_OUT, SLAB), f32)
    for k_z in range(3):
        matrix = []
        for tap in range(9):
            up_part = first_up[k_z * 9 + tap].astype(f32)
            skip_part = first_skip[k_z * 9 + tap].astype(f32)
            matrix.append(jnp.concatenate([up_part, skip_part], axis=0))
        matrix = jnp.concatenate(matrix, axis=0).astype(bf16)
        total = total + lax.dot_general(
            matrix,
            unfolded[:, k_z * FINE : k_z * FINE + SLAB],
            (((0,), (0,)), ((), ())),
            preferred_element_type=f32,
        )
    mean = jnp.sum(total, axis=1, keepdims=True) / SLAB
    deviation = total - mean
    first = jnp.concatenate([deviation[:, :FINE], in_parts(mean)], axis=1).reshape(16, 8, FINE + 128)
    second = jnp.concatenate([deviation[:, FINE:], jnp.zeros((C_OUT, 128), f32)], axis=1)
    partial[...] = jnp.concatenate([first, second.reshape(16, 8, FINE + 128)], axis=1).astype(bf16)


def in_parts(values):
    high = values.astype(bf16).astype(f32)
    middle = (values - high).astype(bf16).astype(f32)
    rest = values - high - middle
    lane = lax.broadcasted_iota(jnp.int32, (values.shape[0], 128), 1)
    return jnp.where(
        lane == 0, high, jnp.where(lane == 1, middle, jnp.where(lane == 2, rest, 0.0))
    )


def first_sum_kernel(parts, pre, stats):
    slab = lax.axis_index("gz")
    both = jnp.sum(parts[...].astype(f32), axis=0)
    total = jnp.concatenate([both[:8, :FINE], both[8:, :FINE]], axis=1)
    total = total + jnp.sum(both[:8, FINE:], axis=1, keepdims=True)
    pre[...] = total
    mean = jnp.sum(total, axis=1, keepdims=True) / SLAB
    deviation = total - mean
    square = jnp.sum(deviation * deviation, axis=1, keepdims=True)
    tail = in_parts(jnp.concatenate([mean, square], axis=0))
    half = FINE // 2
    first = jnp.concatenate([deviation[:, :half], deviation[:, half:FINE]], axis=0)
    last = jnp.concatenate([deviation[:, FINE : FINE + half], deviation[:, FINE + half :]], axis=0)
    first = jnp.concatenate([first, tail], axis=1).astype(bf16)
    last = jnp.concatenate([last, tail], axis=1).astype(bf16)
    for target in range(stats.shape[0]):
        above = target > slab

        @pl.when(above)
        def _():
            stats[target] = last

        @pl.when(jnp.logical_not(above))
        def _():
            stats[target] = first


def first_norm_kernel(pre, stats, packed):
    slab, slabs = lax.axis_index("gz"), stats.shape[0]
    half = FINE // 2
    tails = jnp.sum(stats[:, :, half:].astype(f32), axis=2, keepdims=True)
    means = tails[:, :8]
    mean = jnp.sum(means, axis=0) / slabs
    apart = means - mean[None]
    square = jnp.sum(tails[:, 8:] + SLAB * apart * apart, axis=0)
    inverse = lax.rsqrt(square / (slabs * SLAB) + NORM_EPS)

    def neighbour(index):
        block = stats[index].astype(f32)
        centre = jnp.sum(block[:8, half:], axis=1, keepdims=True)
        return jnp.concatenate([block[:8, :half], block[8:, :half]], axis=1) + centre

    low, high = neighbour(jnp.maximum(slab - 1, 0)), neighbour(jnp.minimum(slab + 1, slabs - 1))
    lower = jnp.concatenate([low, pre[:, :FINE]], axis=1)
    upper = jnp.concatenate([pre[:, FINE:], high], axis=1)
    wide = jnp.broadcast_to(inverse, (8, 128))
    main = wide.astype(bf16).astype(f32)
    block = jnp.concatenate(
        [
            jnp.concatenate([(lower - mean) * inverse, main], axis=1),
            jnp.concatenate([(upper - mean) * inverse, wide - main], axis=1),
        ],
        axis=0,
    ).astype(bf16)
    for target in range(16):
        packed[target] = block


def read_planes(packed, block):
    pair = packed[pl.ds(2 * block, 2), 0:16, :SLAB].astype(f32)
    return jnp.concatenate([pair[:, :8].reshape(16, SLAB), pair[:, 8:].reshape(16, SLAB)], axis=1)


def source_masks(extent):
    cell = lax.broadcasted_iota(jnp.int32, (1, extent), 1)
    column, row = cell % (2 * XC), cell // (2 * XC) % (2 * YC)
    in_x = {-1: jnp.where(column == 2 * XC - 1, 0.0, 1.0), 1: jnp.where(column == 0, 0.0, 1.0)}
    in_y = {-1: jnp.where(row == 2 * YC - 1, 0.0, 1.0), 1: jnp.where(row == 0, 0.0, 1.0)}
    return in_y, in_x


def nine_shifts(values, masks):
    in_y, in_x = masks
    extent = values.shape[-1]
    by_x = {0: values, -1: values * in_x[-1], 1: values * in_x[1]}
    for step_y in (-1, 0, 1):
        for step_x in (-1, 0, 1):
            moved = by_x[step_x] if step_y == 0 else by_x[step_x] * in_y[step_y]
            offset = (-(step_y * 2 * XC + step_x)) % extent
            yield moved if offset == 0 else pltpu.roll(moved, offset, 1)


def unfold_block(values, unfolded, block, sign, masks):
    for place, moved in enumerate(nine_shifts(values, masks)):
        tap = place if sign == 1 else 8 - place
        unfolded[tap, pl.ds(pl.multiple_of(block * 16, 16), 16), :] = moved.astype(bf16)


def tap_matrix(weights, tap, first):
    both = weights[:, tap].astype(f32)
    return both[:, first * 8 : first * 8 + 8].reshape(C_OUT, C_OUT)


def matrix_kernel(weights, first_skip, forward, far_backward, far_first, backward, first, semaphores):
    for tap in range(27):
        at = slice(tap * 128, tap * 128 + 128)
        second = tap_matrix(weights, tap, 0)
        forward[:, at] = jnp.transpose(second).astype(bf16)
        backward[:, at] = second.astype(bf16)
        skip_part = jnp.concatenate([first_skip[tap].astype(f32), jnp.zeros((8, 128), f32)], axis=0)
        first[0:128, at] = tap_matrix(weights, tap, 1).astype(bf16)
        first[128:144, at] = skip_part.astype(bf16)
    for copy in copies((backward, first), (far_backward, far_first), semaphores):
        copy.wait()


def second_conv_kernel(
    packed, matrix, pre, halo, stats, unfolded
):
    mask = edge_mask(lax.axis_index("gz"), stats.shape[0], 1)
    masks = source_masks(HALOED)

    def prepare(block, carry):
        hidden = activate(read_planes(packed, block)).astype(bf16).astype(f32) * mask
        unfold_block(hidden, unfolded, block, 1, masks)
        return carry

    lax.fori_loop(0, 8, prepare, 0)
    total = jnp.zeros((C_OUT, SLAB), f32)
    for k_z in range(3):
        total = total + jnp.dot(
            matrix[:, k_z * 1152 : k_z * 1152 + 1152],
            unfolded[:, :, k_z * FINE : k_z * FINE + SLAB].reshape(1152, SLAB),
            preferred_element_type=f32,
        )
    pre[...] = total
    mean = jnp.sum(total, axis=1, keepdims=True) / SLAB
    deviation = total - mean
    square = jnp.sum(deviation * deviation, axis=1, keepdims=True)
    halo[...] = deviation.astype(bf16)
    row = lax.broadcasted_iota(jnp.int32, (2, 128), 0)
    tile = jnp.where(row < 1, as_row(mean), as_row(square))
    stats[...] = jnp.broadcast_to(tile[None], stats.shape)


def second_norm_kernel(
    pre, low, high, stats, far_cot, decoded, normed, slope, inverse_out, sums, cotangent, semaphores
):
    (fetch,) = copies((far_cot,), (cotangent,), semaphores)
    slab, share = lax.axis_index("gz"), lax.axis_index("ch")
    slabs = stats.shape[0]
    gathered = stats[...]
    means = gathered[:, 0:1]
    mean_row = jnp.sum(means, axis=0) / slabs
    apart = means - mean_row[None]
    square = jnp.sum(gathered[:, 1:2] + SLAB * apart * apart, axis=0)
    inverse_row = lax.rsqrt(square / (slabs * SLAB) + NORM_EPS)
    inverse_out[...] = jnp.broadcast_to(inverse_row, inverse_out.shape)
    below = stats[jnp.maximum(slab - 1, 0)][0:1] - mean_row
    above = stats[jnp.minimum(slab + 1, slabs - 1)][0:1] - mean_row
    mean, inverse = as_column(mean_row), as_column(inverse_row)
    normed[:, :SLAB] = (low[...].astype(f32) + as_column(below)) * inverse
    normed[:, SLAB : 2 * SLAB] = (pre[...] - mean) * inverse
    normed[:, 2 * SLAB :] = (high[...].astype(f32) + as_column(above)) * inverse
    own = normed[pl.ds(pl.multiple_of(share * 8, 8), 8), SLAB : 2 * SLAB]
    decoded[...] = activate(own).astype(bf16)

    def prepare(block, carry):
        at = pl.ds(pl.multiple_of(block * 16, 16), 16)
        pair = cotangent[pl.ds(2 * block, 2)].astype(f32)
        planes = [pair[:, row : row + 8].reshape(16, SLAB) for row in (0, 8, 16)]
        slope[at, :] = jnp.concatenate(planes, axis=1) * activate_slope(normed[at, :])
        return carry

    fetch.wait()
    lax.fori_loop(0, 8, prepare, 0)
    inner = slope[:, SLAB : 2 * SLAB]
    one = as_row(jnp.sum(inner, axis=1, keepdims=True))
    two = as_row(jnp.sum(inner * normed[:, SLAB : 2 * SLAB], axis=1, keepdims=True))
    row = lax.broadcasted_iota(jnp.int32, (2, 128), 0)
    sums[...] = jnp.broadcast_to(jnp.where(row < 1, one, two)[None], sums.shape)


def total_means(sums):
    totals = jnp.sum(sums[...], axis=0) / (sums.shape[0] * SLAB)
    return as_column(totals[0:1]), as_column(totals[1:2])


def second_back_kernel(
    normed, slope, inverse_row, sums_in, packed, far_matrix,
    slope_one, sums, weight_grad,
    unfolded, grads, columns, matrix, own_unfolded, semaphores,
):
    (fetch,) = copies((far_matrix,), (matrix,), semaphores)
    slab, share = lax.axis_index("gz"), lax.axis_index("ch")
    mask = edge_mask(slab, sums.shape[0], 2)
    masks = source_masks(WIDE)
    mean_grad, mean_cross = total_means(sums_in)
    columns[0] = jnp.broadcast_to(mean_grad, (C_OUT, 128))
    columns[1] = jnp.broadcast_to(mean_cross, (C_OUT, 128))
    columns[2] = jnp.broadcast_to(as_column(inverse_row[0:1]), (C_OUT, 128))

    def prepare(block, carry):
        at = pl.ds(pl.multiple_of(block * 16, 16), 16)
        grad = columns[2, at, :1] * (slope[at, :] - columns[0, at, :1] - normed[at, :] * columns[1, at, :1])
        grad = grad.astype(bf16).astype(f32) * mask
        grads[at, :] = grad[:, SLAB : 2 * SLAB]
        unfold_block(grad, unfolded, block, -1, masks)
        return carry

    lax.fori_loop(0, 8, prepare, 0)
    fetch.wait()
    total = jnp.zeros((C_OUT, HALOED), f32)
    for k_z in range(3):
        total = total + jnp.dot(
            matrix[:, k_z * 1152 : k_z * 1152 + 1152],
            unfolded[:, :, (2 - k_z) * FINE : (2 - k_z) * FINE + HALOED].reshape(1152, HALOED),
            preferred_element_type=f32,
        )
    both = packed[:, :, :SLAB].astype(f32)
    first_normed = jnp.concatenate(
        [both[:, :8].reshape(C_OUT, SLAB), both[:, 8:].reshape(C_OUT, SLAB)], axis=1
    )
    whole = total * activate_slope(first_normed)
    slope_one[...] = whole
    inner = whole[:, FINE : 3 * FINE]
    one = as_row(jnp.sum(inner, axis=1, keepdims=True))
    two = as_row(jnp.sum(inner * first_normed[:, FINE : 3 * FINE], axis=1, keepdims=True))
    row = lax.broadcasted_iota(jnp.int32, (2, 128), 0)
    sums[...] = jnp.broadcast_to(jnp.where(row < 1, one, two)[None], sums.shape)
    own = activate(read_planes(packed, share // 2)).astype(bf16).astype(f32)
    own = own * edge_mask(slab, sums.shape[0], 1)
    for tap, moved in enumerate(nine_shifts(own, source_masks(HALOED))):
        own_unfolded[tap * 16 : tap * 16 + 16, :] = moved.astype(bf16)
    odd = share % 2 == 1
    turned = jnp.transpose(grads[...]).astype(bf16)
    for k_z in range(3):
        product = jnp.dot(
            own_unfolded[:, k_z * FINE : k_z * FINE + SLAB], turned, preferred_element_type=f32
        ).reshape(9, 2, 8, 128)
        weight_grad[k_z * 72 : k_z * 72 + 72, :] = jnp.where(odd, product[:, 1], product[:, 0]).reshape(72, 128)


def first_back_kernel(
    slope, sums_in, packed, far_matrix, up_weight, coarse, joined, second_grad,
    skip_grad, coarse_own, coarse_next, weight_grads,
    unfolded, grads, columns, spread, up_matrix, matrix, own_unfolded, semaphores,
):
    (fetch,) = copies((far_matrix,), (matrix,), semaphores)
    slab = lax.axis_index("gz")
    mask = edge_mask(slab, sums_in.shape[0], 1)
    masks = source_masks(HALOED)
    mean_grad, mean_cross = total_means(sums_in)
    columns[0] = jnp.broadcast_to(mean_grad, (C_OUT, 128))
    columns[1] = jnp.broadcast_to(mean_cross, (C_OUT, 128))
    wide = packed[:, :, SLAB:].astype(f32)
    columns[2] = (wide[:, :8] + wide[:, 8:]).reshape(C_OUT, 128)

    def prepare(block, carry):
        at = pl.ds(pl.multiple_of(block * 16, 16), 16)
        normed = read_planes(packed, block)
        grad = columns[2, at, :1] * (slope[at, :] - columns[0, at, :1] - normed * columns[1, at, :1])
        grad = grad.astype(bf16).astype(f32) * mask
        grads[at, :] = grad[:, FINE : 3 * FINE]
        unfold_block(grad, unfolded, block, -1, masks)
        return carry

    lax.fori_loop(0, 8, prepare, 0)
    fetch.wait()
    total = jnp.zeros((144, SLAB), f32)
    for k_z in range(3):
        total = total + jnp.dot(
            matrix[:, k_z * 1152 : k_z * 1152 + 1152],
            unfolded[:, :, (2 - k_z) * FINE : (2 - k_z) * FINE + SLAB].reshape(1152, SLAB),
            preferred_element_type=f32,
        )
    skip_grad[...] = total[128:136].astype(bf16)
    d_up = jnp.concatenate([total[:128, :FINE], total[:128, FINE:]], axis=0).astype(bf16)
    last = (((1,), (1,)), ((), ()))
    parted = jnp.dot(d_up, interleave_matrix(True), preferred_element_type=f32)
    for y_par in (0, 1):
        for x_par in (0, 1):
            at = (y_par * 2 + x_par) * COARSE
            source = jnp.concatenate(
                [parted[:128, at : at + COARSE], parted[128:, at : at + COARSE]], axis=1
            )
            for k_y, y_off in PARITY[y_par]:
                for k_x, x_off in PARITY[x_par]:
                    tap = k_y * 3 + k_x
                    spread[tap * 128 : tap * 128 + 128, :] = coarse_shift(
                        source, -y_off, -x_off
                    ).astype(bf16)
    for tap in range(27):
        at = (tap // 9) * 1152 + (tap % 9) * 128
        up_matrix[:, at : at + 128] = up_weight[tap]
    low_plane, high_plane = spread[:, :COARSE], spread[:, COARSE:]
    coarse_own[...] = jnp.dot(
        up_matrix[:, 1152:2304], low_plane, preferred_element_type=f32
    ) + jnp.dot(up_matrix[:, 2304:], high_plane, preferred_element_type=f32)
    coarse_next[...] = jnp.dot(up_matrix[:, :1152], high_plane, preferred_element_type=f32)
    here, following = coarse[0], coarse[1]
    for k_z, source, plane in ((0, following, high_plane), (1, here, low_plane), (2, here, high_plane)):
        product = lax.dot_general(source, plane, last, preferred_element_type=f32)
        for tap in range(9):
            at = (k_z * 9 + tap) * 16
            weight_grads[at : at + 16, :] = product[:, tap * 128 : tap * 128 + 128].astype(bf16)
    own = joined[...].astype(f32)
    for tap, moved in enumerate(nine_shifts(own, masks)):
        own_unfolded[tap * 16 : tap * 16 + 16, :] = moved.astype(bf16)
    turned = jnp.transpose(grads[...]).astype(bf16)
    for k_z in range(3):
        product = jnp.dot(
            own_unfolded[:, k_z * FINE : k_z * FINE + SLAB], turned, preferred_element_type=f32
        )
        weight_grads[432 + k_z * 144 : 576 + k_z * 144, :] = product.astype(bf16)
    rest = jnp.concatenate([second_grad[...], jnp.zeros((GRAD_ROWS - 1080, 128), f32)], axis=0)
    weight_grads[864:, :] = rest.astype(bf16)


def grad_sum_kernel(parts, spread):
    total = jnp.sum(parts[...].astype(f32), axis=0) * (1.0 / math.sqrt(SLAB))
    spread[...] = jnp.broadcast_to(total.astype(bf16)[None], spread.shape)


def grad_split_kernel(gathered, up, first_up, first_skip, second):
    values = gathered[...].reshape(GRAD_ROWS, 128).astype(f32)
    up[...] = values[:432].reshape(27, 16, 128)
    first = values[432:864].reshape(27, 16, 128)
    first_up[...] = first[:, :8]
    first_skip[...] = first[:, 8:]
    second[...] = values[864:1080].reshape(27, 8, 128)


def local(coarse, encoder_skip, up_weight, first_up, first_skip, second_weight, cotangent):
    slabs, shares = lax.axis_size("gz"), lax.axis_size("ch")
    upward = [(i, i + 1) for i in range(slabs - 1)]
    downward = [(i + 1, i) for i in range(slabs - 1)]

    def from_below(block):
        return lax.ppermute(block, "gz", upward)

    def from_above(block):
        return lax.ppermute(block, "gz", downward)

    def swap(block, axis):
        return lax.all_to_all(block, axis, 0, 0, tiled=True)

    def io_major(weight):
        return jnp.transpose(weight, (0, 2, 1))

    up_own, up_first = io_major(up_weight), io_major(first_up)
    skip_first, second_own = io_major(first_skip), io_major(second_weight)

    here = coarse.reshape(16, COARSE)
    halo = ((8, 2 * COARSE + 3 * FINE), bf16)
    upper, lower, own_skip, own_cot = call(
        halo_kernel,
        [halo, halo, ((8, SLAB), bf16), ((8, SLAB), bf16)],
        (here, encoder_skip, cotangent),
        [
            pltpu.VMEM((16, COARSE), bf16), pltpu.VMEM((8, 2, FINE), bf16), pltpu.VMEM((8, 2, FINE), bf16),
            pltpu.SemaphoreType.DMA((3,)),
        ],
        far=(0, 1, 2),
    )
    low, high = from_below(upper), from_above(lower)
    pieces = jnp.transpose(up_weight.reshape(27, 16, 8, 16), (1, 3, 0, 2)).reshape(16, 16, 216)
    mixed, pair, cot_planes = call(
        mix_kernel,
        [((16, 16, 640), bf16), ((2, 16, COARSE), bf16), ((32, SLAB), bf16)],
        (pieces, here, low, high, own_cot),
    )
    mixed, second_own, up_shared = lax.optimization_barrier((mixed, second_own, up_first))
    kernels = lax.all_gather(jnp.concatenate([second_own, up_shared], axis=1), "ch", axis=0)
    cot_planes = lax.all_gather(cot_planes, "ch", axis=0)

    partial, joined = call(
        up_kernel,
        [((16, 16, FINE + 128), bf16), ((16, HALOED), bf16)],
        (swap(mixed, "ch"), own_skip, low, high, up_first, skip_first),
        [pltpu.VMEM((144, HALOED), bf16)],
        near_outs=(1,),
    )
    pre, stats = call(
        first_sum_kernel,
        [((8, SLAB), f32), ((slabs, 16, FINE // 2 + 128), bf16)],
        (swap(partial, "ch"),),
    )
    (packed,) = call(
        first_norm_kernel, [((16, 16, SLAB + 128), bf16)], (pre, swap(stats, "gz"))
    )
    packed, kernels = lax.optimization_barrier((packed, kernels))
    packed = swap(packed, "ch")
    forward, backward, first = call(
        matrix_kernel,
        [((128, 3456), bf16), ((128, 3456), bf16), ((144, 3456), bf16)],
        (kernels, skip_first),
        [pltpu.VMEM((128, 3456), bf16), pltpu.VMEM((144, 3456), bf16), pltpu.SemaphoreType.DMA((2,))],
        far_outs=(1, 2),
        near_outs=(0,),
    )
    unfolded = pltpu.VMEM((9, 128, HALOED), bf16)
    second_pre, halo, stats = call(
        second_conv_kernel,
        [
            ((128, SLAB), f32), ((128, SLAB), bf16), ((slabs, 2, 128), f32),
        ],
        (packed, forward),
        [unfolded],
        14,
        near=(1,),
        near_outs=(0, 1),
    )
    decoded, normed, slope, inverse, sums = call(
        second_norm_kernel,
        [
            ((8, SLAB), bf16), ((128, WIDE), f32), ((128, WIDE), f32), ((8, 128), f32),
            ((slabs, 2, 128), f32),
        ],
        (second_pre, from_below(halo), from_above(halo), swap(stats, "gz"), cot_planes),
        [pltpu.VMEM((16, 32, SLAB), bf16), pltpu.SemaphoreType.DMA((1,))],
        far=(4,),
        near=(0,),
        near_outs=(1, 2),
    )
    slope_one, sums, second_grad = call(
        second_back_kernel,
        [
            ((128, HALOED), f32), ((slabs, 2, 128), f32), ((216, 128), f32),
        ],
        (
            normed, slope, inverse, swap(sums, "gz"), packed, backward,
        ),
        [
            pltpu.VMEM((9, 128, WIDE), bf16), pltpu.VMEM((128, SLAB), f32), pltpu.VMEM((3, 128, 128), f32),
            pltpu.VMEM((128, 3456), bf16), pltpu.VMEM((144, HALOED), bf16), pltpu.SemaphoreType.DMA((1,)),
        ],
        20,
        far=(5,),
        near=(0, 1),
        near_outs=(0, 2),
    )
    skip_grad, coarse_own, coarse_next, weight_grads = call(
        first_back_kernel,
        [((8, SLAB), bf16), ((16, COARSE), f32), ((16, COARSE), f32), ((GRAD_ROWS, 128), bf16)],
        (
            slope_one, swap(sums, "gz"), packed, first,
            up_own, pair, joined, second_grad,
        ),
        [
            unfolded, pltpu.VMEM((128, SLAB), f32), pltpu.VMEM((3, 128, 128), f32),
            pltpu.VMEM((1152, 2 * COARSE), bf16), pltpu.VMEM((16, 3456), bf16),
            pltpu.VMEM((144, 3456), bf16), pltpu.VMEM((144, HALOED), bf16), pltpu.SemaphoreType.DMA((1,)),
        ],
        17,
        far=(3,),
        near=(0, 6, 7),
    )
    coarse_grad = (coarse_own + from_below(coarse_next)).astype(bf16)
    rows = GRAD_ROWS // slabs
    (spread,) = call(
        grad_sum_kernel,
        [((slabs, rows, 128), bf16)],
        (swap(weight_grads.reshape(slabs, rows, 128), "gz"),),
    )
    grads = call(
        grad_split_kernel,
        [((27, 16, 128), f32), ((27, 8, 128), f32), ((27, 8, 128), f32), ((27, 8, 128), f32)],
        (swap(spread, "gz"),),
    )
    grads = [jnp.transpose(grad, (0, 2, 1)) for grad in grads]
    return (
        decoded.reshape(8, 2, FINE),
        coarse_grad.reshape(16, 1, COARSE),
        skip_grad.reshape(8, 2, FINE),
        *grads,
    )


def solution(mesh):
    volume, kernel = P("ch", "gz", None), P(None, None, "ch")
    return jax.shard_map(
        local,
        mesh=mesh,
        in_specs=(volume, volume, kernel, kernel, kernel, kernel, volume),
        out_specs=(volume, volume, volume, kernel, kernel, kernel, kernel),
        check_vma=False,
    )
```

```python
import math

import jax
import jax.numpy as jnp
from jax import lax
from jax.experimental import pallas as pl
from jax.experimental.pallas import tpu as pltpu
from jax.sharding import PartitionSpec as P

C_OUT = 128
XC = 16
YC = 8
COARSE = YC * XC
FINE = 4 * COARSE
SLAB = 2 * FINE
HALOED = 4 * FINE
WIDE = 6 * FINE
LEAK_SLOPE = 0.01
KINK_WIDTH = 0.01
NORM_EPS = 1e-05
PARITY = (((1, 0),), ((2, 0), (0, 1)))
GRAD_ROWS = 1280

f32 = jnp.float32
bf16 = jnp.bfloat16


def activate(u):
    q = u * u + KINK_WIDTH
    return 0.5 * (1.0 + LEAK_SLOPE) * u + 0.5 * (1.0 - LEAK_SLOPE) * (q * lax.rsqrt(q))


def activate_slope(u):
    return 0.5 * (1.0 + LEAK_SLOPE) + 0.5 * (1.0 - LEAK_SLOPE) * (
        u * lax.rsqrt(u * u + KINK_WIDTH)
    )


def shift(values, step_y, step_x, rows, columns):
    if step_y == 0 and step_x == 0:
        return values
    extent = values.shape[-1]
    cell = lax.broadcasted_iota(jnp.int32, (1, extent), 1)
    column = cell % columns + step_x
    row = cell // columns % rows + step_y
    inside = (column >= 0) & (column < columns) & (row >= 0) & (row < rows)
    moved = pltpu.roll(values, (-(step_y * columns + step_x)) % extent, 1)
    return moved * jnp.where(inside, 1.0, 0.0)


def coarse_shift(values, step_y, step_x):
    return shift(values, step_y, step_x, YC, XC)


def interleave_matrix(transposed):
    fine_dim = 0 if transposed else 1
    cell = lax.broadcasted_iota(jnp.int32, (FINE, FINE), fine_dim)
    other = lax.broadcasted_iota(jnp.int32, (FINE, FINE), 1 - fine_dim)
    y, x = cell // (2 * XC), cell % (2 * XC)
    source = ((y % 2) * 2 + x % 2) * COARSE + (y // 2) * XC + x // 2
    return jnp.where(source == other, 1.0, 0.0).astype(bf16)


def edge_mask(slab, slabs, width):
    plane = lax.broadcasted_iota(jnp.int32, (1, SLAB + 2 * width * FINE), 1) // FINE
    outside = ((plane < width) & (slab == 0)) | ((plane > width + 1) & (slab == slabs - 1))
    return jnp.where(outside, 0.0, 1.0)


def as_row(column):
    return jnp.transpose(jnp.broadcast_to(column, (C_OUT, C_OUT)))[:1]


def as_column(row):
    return jnp.transpose(jnp.broadcast_to(row, (C_OUT, C_OUT)))[:, :1]


def call(kernel, outs, args, scratch=(), megabytes=8, far=(), far_outs=(), near=(), near_outs=()):
    args = list(args)
    for index in far:
        args[index] = pltpu.with_memory_space_constraint(args[index], pltpu.HBM)
    for index in near:
        args[index] = pltpu.with_memory_space_constraint(args[index], pltpu.VMEM)

    def spec(index, which):
        return pl.BlockSpec(memory_space=pltpu.HBM if index in which else pltpu.VMEM)

    def out(index, shape, dtype):
        if index in far_outs:
            return pltpu.HBM(shape, dtype)
        return pltpu.VMEM(shape, dtype) if index in near_outs else jax.ShapeDtypeStruct(shape, dtype)

    return pl.pallas_call(
        kernel,
        out_shape=[out(index, *shape) for index, shape in enumerate(outs)],
        in_specs=[spec(index, far) for index in range(len(args))],
        out_specs=[spec(index, far_outs) for index in range(len(outs))],
        scratch_shapes=list(scratch),
        compiler_params=pltpu.CompilerParams(vmem_limit_bytes=megabytes * 2**20),
    )(*args)


def copies(sources, targets, semaphores):
    started = []
    for index, (source, target) in enumerate(zip(sources, targets)):
        copy = pltpu.make_async_copy(source, target, semaphores.at[index])
        copy.start()
        started.append(copy)
    return started


def halo_kernel(
    far_coarse, far_skip, far_cot, upward, downward, own_skip, own_cot, coarse, skip, cotangent, semaphores
):
    for copy in copies((far_coarse, far_skip, far_cot), (coarse, skip, cotangent), semaphores):
        copy.wait()
    cells = coarse[...].astype(f32)
    cells = [cells[:8], cells[8:]]
    skip_planes, cot_planes = skip[...].astype(f32), cotangent[...].astype(f32)
    both = [cot_planes[:, 0], cot_planes[:, 1]]
    upward[...] = jnp.concatenate(cells + [skip_planes[:, 1]] + both, axis=1).astype(bf16)
    downward[...] = jnp.concatenate(cells + [skip_planes[:, 0]] + both, axis=1).astype(bf16)
    own_skip[...] = jnp.concatenate([skip_planes[:, 0], skip_planes[:, 1]], axis=1).astype(bf16)
    own_cot[...] = jnp.concatenate(both, axis=1).astype(bf16)


def mix_kernel(pieces, coarse, low, high, own_cot, mixed, pair, cot_planes):
    below, above = low[...].astype(f32), high[...].astype(f32)
    here = coarse[...].astype(f32)
    before = jnp.concatenate([below[:, :COARSE], below[:, COARSE : 2 * COARSE]], axis=0)
    after = jnp.concatenate([above[:, :COARSE], above[:, COARSE : 2 * COARSE]], axis=0)
    planes = jnp.concatenate([before, here, after], axis=1).astype(bf16)
    mixed[:, :, :256] = jnp.zeros((16, 16, 256), bf16)
    for target in range(16):
        mixed[target, :, :216] = pieces[target]
        mixed[target, :, 256:] = planes
    pair[0] = coarse[...]
    pair[1] = after.astype(bf16)
    cot = own_cot[...].astype(f32)
    at = 2 * COARSE + FINE
    slabs = [below[:, at:], cot, above[:, at:], jnp.zeros((8, SLAB), f32)]
    cot_planes[...] = jnp.concatenate(slabs, axis=0).astype(bf16)


def up_kernel(mixed, own_skip, low, high, first_up, first_skip, partial, joined, unfolded):
    slab = lax.axis_index("gz")
    packed = mixed[...]
    weights = packed[:, :, :256].reshape(256, 256)
    mixture = []
    for plane in range(3):
        source = packed[:, :, 256 + plane * COARSE : 256 + (plane + 1) * COARSE].reshape(256, COARSE)
        mixture.append(
            lax.dot_general(weights, source, (((0,), (0,)), ((), ())), preferred_element_type=f32)
        )
    rows = []
    for sources in (((2, 0), (0, 1)), ((1, 1),), ((2, 1), (0, 2)), ((1, 2),)):
        cells = []
        for y_par in (0, 1):
            for x_par in (0, 1):
                total = None
                for k_z, plane in sources:
                    for k_y, y_off in PARITY[y_par]:
                        for k_x, x_off in PARITY[x_par]:
                            tap = k_z * 9 + k_y * 3 + k_x
                            term = coarse_shift(mixture[plane][tap * 8 : tap * 8 + 8], y_off, x_off)
                            total = term if total is None else total + term
                cells.append(total)
        rows.append(jnp.concatenate(cells, axis=1))
    spread = jnp.concatenate(rows, axis=0).astype(bf16)
    fine = jnp.dot(spread, interleave_matrix(False), preferred_element_type=f32)
    first_inside = jnp.where(slab == 0, 0.0, 1.0)
    upsampled = jnp.concatenate(
        [fine[0:8] * first_inside, fine[8:16], fine[16:24], fine[24:32]], axis=1
    )
    skip_at = slice(2 * COARSE, 2 * COARSE + FINE)
    skip = jnp.concatenate(
        [low[:, skip_at].astype(f32), own_skip[...].astype(f32), high[:, skip_at].astype(f32)], axis=1
    )
    features = jnp.concatenate([upsampled, skip], axis=0)
    joined[...] = features.astype(bf16)
    for tap, moved in enumerate(nine_shifts(features, source_masks(HALOED))):
        unfolded[tap * 16 : tap * 16 + 16, :] = moved.astype(bf16)
    total = jnp.zeros((C_OUT, SLAB), f32)
    for k_z in range(3):
        matrix = []
        for tap in range(9):
            up_part = first_up[k_z * 9 + tap].astype(f32)
            skip_part = first_skip[k_z * 9 + tap].astype(f32)
            matrix.append(jnp.concatenate([up_part, skip_part], axis=0))
        matrix = jnp.concatenate(matrix, axis=0).astype(bf16)
        total = total + lax.dot_general(
            matrix,
            unfolded[:, k_z * FINE : k_z * FINE + SLAB],
            (((0,), (0,)), ((), ())),
            preferred_element_type=f32,
        )
    mean = jnp.sum(total, axis=1, keepdims=True) / SLAB
    deviation = total - mean
    first = jnp.concatenate([deviation[:, :FINE], in_parts(mean)], axis=1).reshape(16, 8, FINE + 128)
    second = jnp.concatenate([deviation[:, FINE:], jnp.zeros((C_OUT, 128), f32)], axis=1)
    partial[...] = jnp.concatenate([first, second.reshape(16, 8, FINE + 128)], axis=1).astype(bf16)


def in_parts(values):
    high = values.astype(bf16).astype(f32)
    middle = (values - high).astype(bf16).astype(f32)
    rest = values - high - middle
    lane = lax.broadcasted_iota(jnp.int32, (values.shape[0], 128), 1)
    return jnp.where(
        lane == 0, high, jnp.where(lane == 1, middle, jnp.where(lane == 2, rest, 0.0))
    )


def first_sum_kernel(parts, pre, stats):
    slab = lax.axis_index("gz")
    both = jnp.sum(parts[...].astype(f32), axis=0)
    total = jnp.concatenate([both[:8, :FINE], both[8:, :FINE]], axis=1)
    total = total + jnp.sum(both[:8, FINE:], axis=1, keepdims=True)
    pre[...] = total
    mean = jnp.sum(total, axis=1, keepdims=True) / SLAB
    deviation = total - mean
    square = jnp.sum(deviation * deviation, axis=1, keepdims=True)
    tail = in_parts(jnp.concatenate([mean, square], axis=0))
    half = FINE // 2
    first = jnp.concatenate([deviation[:, :half], deviation[:, half:FINE]], axis=0)
    last = jnp.concatenate([deviation[:, FINE : FINE + half], deviation[:, FINE + half :]], axis=0)
    first = jnp.concatenate([first, tail], axis=1).astype(bf16)
    last = jnp.concatenate([last, tail], axis=1).astype(bf16)
    for target in range(stats.shape[0]):
        above = target > slab

        @pl.when(above)
        def _():
            stats[target] = last

        @pl.when(jnp.logical_not(above))
        def _():
            stats[target] = first


def first_norm_kernel(pre, stats, packed):
    slab, slabs = lax.axis_index("gz"), stats.shape[0]
    half = FINE // 2
    tails = jnp.sum(stats[:, :, half:].astype(f32), axis=2, keepdims=True)
    means = tails[:, :8]
    mean = jnp.sum(means, axis=0) / slabs
    apart = means - mean[None]
    square = jnp.sum(tails[:, 8:] + SLAB * apart * apart, axis=0)
    inverse = lax.rsqrt(square / (slabs * SLAB) + NORM_EPS)

    def neighbour(index):
        block = stats[index].astype(f32)
        centre = jnp.sum(block[:8, half:], axis=1, keepdims=True)
        return jnp.concatenate([block[:8, :half], block[8:, :half]], axis=1) + centre

    low, high = neighbour(jnp.maximum(slab - 1, 0)), neighbour(jnp.minimum(slab + 1, slabs - 1))
    lower = jnp.concatenate([low, pre[:, :FINE]], axis=1)
    upper = jnp.concatenate([pre[:, FINE:], high], axis=1)
    wide = jnp.broadcast_to(inverse, (8, 128))
    main = wide.astype(bf16).astype(f32)
    block = jnp.concatenate(
        [
            jnp.concatenate([(lower - mean) * inverse, main], axis=1),
            jnp.concatenate([(upper - mean) * inverse, wide - main], axis=1),
        ],
        axis=0,
    ).astype(bf16)
    for target in range(16):
        packed[target] = block


def read_planes(packed, block):
    pair = packed[pl.ds(2 * block, 2), 0:16, :SLAB].astype(f32)
    return jnp.concatenate([pair[:, :8].reshape(16, SLAB), pair[:, 8:].reshape(16, SLAB)], axis=1)


def source_masks(extent):
    cell = lax.broadcasted_iota(jnp.int32, (1, extent), 1)
    column, row = cell % (2 * XC), cell // (2 * XC) % (2 * YC)
    in_x = {-1: jnp.where(column == 2 * XC - 1, 0.0, 1.0), 1: jnp.where(column == 0, 0.0, 1.0)}
    in_y = {-1: jnp.where(row == 2 * YC - 1, 0.0, 1.0), 1: jnp.where(row == 0, 0.0, 1.0)}
    return in_y, in_x


def nine_shifts(values, masks):
    in_y, in_x = masks
    extent = values.shape[-1]
    by_x = {0: values, -1: values * in_x[-1], 1: values * in_x[1]}
    for step_y in (-1, 0, 1):
        for step_x in (-1, 0, 1):
            moved = by_x[step_x] if step_y == 0 else by_x[step_x] * in_y[step_y]
            offset = (-(step_y * 2 * XC + step_x)) % extent
            yield moved if offset == 0 else pltpu.roll(moved, offset, 1)


def unfold_block(values, unfolded, block, sign, masks):
    for place, moved in enumerate(nine_shifts(values, masks)):
        tap = place if sign == 1 else 8 - place
        unfolded[tap, pl.ds(pl.multiple_of(block * 16, 16), 16), :] = moved.astype(bf16)


def tap_matrix(weights, tap, first):
    both = weights[:, tap].astype(f32)
    return both[:, first * 8 : first * 8 + 8].reshape(C_OUT, C_OUT)


def matrix_kernel(
    weights, first_skip, up_weight, joined,
    forward, far_backward, far_first, far_up, far_interleave, far_unfolded,
    backward, first, up_matrix, interleave, unfolded, semaphores,
):
    for tap in range(27):
        at = slice(tap * 128, tap * 128 + 128)
        second = tap_matrix(weights, tap, 0)
        forward[:, at] = jnp.transpose(second).astype(bf16)
        backward[:, at] = second.astype(bf16)
        skip_part = jnp.concatenate([first_skip[tap].astype(f32), jnp.zeros((8, 128), f32)], axis=0)
        first[0:128, at] = tap_matrix(weights, tap, 1).astype(bf16)
        first[128:144, at] = skip_part.astype(bf16)
    for tap in range(27):
        at = (tap // 9) * 1152 + (tap % 9) * 128
        up_matrix[:, at : at + 128] = up_weight[tap]
    interleave[...] = interleave_matrix(True)
    for tap, moved in enumerate(nine_shifts(joined[...].astype(f32), source_masks(HALOED))):
        unfolded[tap * 16 : tap * 16 + 16, :] = moved.astype(bf16)
    made = (backward, first, up_matrix, interleave, unfolded)
    kept = (far_backward, far_first, far_up, far_interleave, far_unfolded)
    for copy in copies(made, kept, semaphores):
        copy.wait()


def second_conv_kernel(
    packed, matrix, pre, halo, stats, unfolded
):
    mask = edge_mask(lax.axis_index("gz"), stats.shape[0], 1)
    masks = source_masks(HALOED)

    def prepare(block, carry):
        hidden = activate(read_planes(packed, block)).astype(bf16).astype(f32) * mask
        unfold_block(hidden, unfolded, block, 1, masks)
        return carry

    lax.fori_loop(0, 8, prepare, 0)
    total = jnp.zeros((C_OUT, SLAB), f32)
    for k_z in range(3):
        total = total + jnp.dot(
            matrix[:, k_z * 1152 : k_z * 1152 + 1152],
            unfolded[:, :, k_z * FINE : k_z * FINE + SLAB].reshape(1152, SLAB),
            preferred_element_type=f32,
        )
    pre[...] = total
    mean = jnp.sum(total, axis=1, keepdims=True) / SLAB
    deviation = total - mean
    square = jnp.sum(deviation * deviation, axis=1, keepdims=True)
    halo[...] = deviation.astype(bf16)
    row = lax.broadcasted_iota(jnp.int32, (2, 128), 0)
    tile = jnp.where(row < 1, as_row(mean), as_row(square))
    stats[...] = jnp.broadcast_to(tile[None], stats.shape)


def second_norm_kernel(
    pre, low, high, stats, far_cot, decoded, normed, slope, inverse_out, sums, cotangent, semaphores
):
    (fetch,) = copies((far_cot,), (cotangent,), semaphores)
    slab, share = lax.axis_index("gz"), lax.axis_index("ch")
    slabs = stats.shape[0]
    gathered = stats[...]
    means = gathered[:, 0:1]
    mean_row = jnp.sum(means, axis=0) / slabs
    apart = means - mean_row[None]
    square = jnp.sum(gathered[:, 1:2] + SLAB * apart * apart, axis=0)
    inverse_row = lax.rsqrt(square / (slabs * SLAB) + NORM_EPS)
    inverse_out[...] = jnp.broadcast_to(inverse_row, inverse_out.shape)
    below = stats[jnp.maximum(slab - 1, 0)][0:1] - mean_row
    above = stats[jnp.minimum(slab + 1, slabs - 1)][0:1] - mean_row
    mean, inverse = as_column(mean_row), as_column(inverse_row)
    normed[:, :SLAB] = (low[...].astype(f32) + as_column(below)) * inverse
    normed[:, SLAB : 2 * SLAB] = (pre[...] - mean) * inverse
    normed[:, 2 * SLAB :] = (high[...].astype(f32) + as_column(above)) * inverse
    own = normed[pl.ds(pl.multiple_of(share * 8, 8), 8), SLAB : 2 * SLAB]
    decoded[...] = activate(own).astype(bf16)

    def prepare(block, carry):
        at = pl.ds(pl.multiple_of(block * 16, 16), 16)
        pair = cotangent[pl.ds(2 * block, 2)].astype(f32)
        planes = [pair[:, row : row + 8].reshape(16, SLAB) for row in (0, 8, 16)]
        slope[at, :] = jnp.concatenate(planes, axis=1) * activate_slope(normed[at, :])
        return carry

    fetch.wait()
    lax.fori_loop(0, 8, prepare, 0)
    inner = slope[:, SLAB : 2 * SLAB]
    one = as_row(jnp.sum(inner, axis=1, keepdims=True))
    two = as_row(jnp.sum(inner * normed[:, SLAB : 2 * SLAB], axis=1, keepdims=True))
    row = lax.broadcasted_iota(jnp.int32, (2, 128), 0)
    sums[...] = jnp.broadcast_to(jnp.where(row < 1, one, two)[None], sums.shape)


def total_means(sums):
    totals = jnp.sum(sums[...], axis=0) / (sums.shape[0] * SLAB)
    return as_column(totals[0:1]), as_column(totals[1:2])


def second_back_kernel(
    normed, slope, inverse_row, sums_in, packed, far_matrix,
    slope_one, sums, weight_grad,
    unfolded, grads, columns, matrix, own_unfolded, semaphores,
):
    (fetch,) = copies((far_matrix,), (matrix,), semaphores)
    slab, share = lax.axis_index("gz"), lax.axis_index("ch")
    mask = edge_mask(slab, sums.shape[0], 2)
    masks = source_masks(WIDE)
    mean_grad, mean_cross = total_means(sums_in)
    columns[0] = jnp.broadcast_to(mean_grad, (C_OUT, 128))
    columns[1] = jnp.broadcast_to(mean_cross, (C_OUT, 128))
    columns[2] = jnp.broadcast_to(as_column(inverse_row[0:1]), (C_OUT, 128))

    def prepare(block, carry):
        at = pl.ds(pl.multiple_of(block * 16, 16), 16)
        grad = columns[2, at, :1] * (slope[at, :] - columns[0, at, :1] - normed[at, :] * columns[1, at, :1])
        grad = grad.astype(bf16).astype(f32) * mask
        grads[at, :] = grad[:, SLAB : 2 * SLAB]
        unfold_block(grad, unfolded, block, -1, masks)
        return carry

    lax.fori_loop(0, 8, prepare, 0)
    fetch.wait()
    total = jnp.zeros((C_OUT, HALOED), f32)
    for k_z in range(3):
        total = total + jnp.dot(
            matrix[:, k_z * 1152 : k_z * 1152 + 1152],
            unfolded[:, :, (2 - k_z) * FINE : (2 - k_z) * FINE + HALOED].reshape(1152, HALOED),
            preferred_element_type=f32,
        )
    both = packed[:, :, :SLAB].astype(f32)
    first_normed = jnp.concatenate(
        [both[:, :8].reshape(C_OUT, SLAB), both[:, 8:].reshape(C_OUT, SLAB)], axis=1
    )
    whole = total * activate_slope(first_normed)
    slope_one[...] = whole
    inner = whole[:, FINE : 3 * FINE]
    one = as_row(jnp.sum(inner, axis=1, keepdims=True))
    two = as_row(jnp.sum(inner * first_normed[:, FINE : 3 * FINE], axis=1, keepdims=True))
    row = lax.broadcasted_iota(jnp.int32, (2, 128), 0)
    sums[...] = jnp.broadcast_to(jnp.where(row < 1, one, two)[None], sums.shape)
    own = activate(read_planes(packed, share // 2)).astype(bf16).astype(f32)
    own = own * edge_mask(slab, sums.shape[0], 1)
    for tap, moved in enumerate(nine_shifts(own, source_masks(HALOED))):
        own_unfolded[tap * 16 : tap * 16 + 16, :] = moved.astype(bf16)
    odd = share % 2 == 1
    turned = jnp.transpose(grads[...]).astype(bf16)
    for k_z in range(3):
        product = jnp.dot(
            own_unfolded[:, k_z * FINE : k_z * FINE + SLAB], turned, preferred_element_type=f32
        ).reshape(9, 2, 8, 128)
        weight_grad[k_z * 72 : k_z * 72 + 72, :] = jnp.where(odd, product[:, 1], product[:, 0]).reshape(72, 128)


def first_back_kernel(
    slope, sums_in, packed, far_matrix, far_up, coarse, far_unfolded, second_grad, far_interleave,
    skip_grad, coarse_own, coarse_next, weight_grads,
    unfolded, grads, columns, spread, up_matrix, matrix, own_unfolded, interleave, semaphores,
):
    kept = (far_matrix, far_up, far_unfolded, far_interleave)
    fetches = copies(kept, (matrix, up_matrix, own_unfolded, interleave), semaphores)
    slab = lax.axis_index("gz")
    mask = edge_mask(slab, sums_in.shape[0], 1)
    masks = source_masks(HALOED)
    mean_grad, mean_cross = total_means(sums_in)
    columns[0] = jnp.broadcast_to(mean_grad, (C_OUT, 128))
    columns[1] = jnp.broadcast_to(mean_cross, (C_OUT, 128))
    wide = packed[:, :, SLAB:].astype(f32)
    columns[2] = (wide[:, :8] + wide[:, 8:]).reshape(C_OUT, 128)

    def prepare(block, carry):
        at = pl.ds(pl.multiple_of(block * 16, 16), 16)
        normed = read_planes(packed, block)
        grad = columns[2, at, :1] * (slope[at, :] - columns[0, at, :1] - normed * columns[1, at, :1])
        grad = grad.astype(bf16).astype(f32) * mask
        grads[at, :] = grad[:, FINE : 3 * FINE]
        unfold_block(grad, unfolded, block, -1, masks)
        return carry

    lax.fori_loop(0, 8, prepare, 0)
    for copy in fetches:
        copy.wait()
    total = jnp.zeros((144, SLAB), f32)
    for k_z in range(3):
        total = total + jnp.dot(
            matrix[:, k_z * 1152 : k_z * 1152 + 1152],
            unfolded[:, :, (2 - k_z) * FINE : (2 - k_z) * FINE + SLAB].reshape(1152, SLAB),
            preferred_element_type=f32,
        )
    skip_grad[...] = total[128:136].astype(bf16)
    d_up = jnp.concatenate([total[:128, :FINE], total[:128, FINE:]], axis=0).astype(bf16)
    last = (((1,), (1,)), ((), ()))
    parted = jnp.dot(d_up, interleave[...], preferred_element_type=f32)
    for y_par in (0, 1):
        for x_par in (0, 1):
            at = (y_par * 2 + x_par) * COARSE
            source = jnp.concatenate(
                [parted[:128, at : at + COARSE], parted[128:, at : at + COARSE]], axis=1
            )
            for k_y, y_off in PARITY[y_par]:
                for k_x, x_off in PARITY[x_par]:
                    tap = k_y * 3 + k_x
                    spread[tap * 128 : tap * 128 + 128, :] = coarse_shift(
                        source, -y_off, -x_off
                    ).astype(bf16)
    low_plane, high_plane = spread[:, :COARSE], spread[:, COARSE:]
    coarse_own[...] = jnp.dot(
        up_matrix[:, 1152:2304], low_plane, preferred_element_type=f32
    ) + jnp.dot(up_matrix[:, 2304:], high_plane, preferred_element_type=f32)
    coarse_next[...] = jnp.dot(up_matrix[:, :1152], high_plane, preferred_element_type=f32)
    here, following = coarse[0], coarse[1]
    for k_z, source, plane in ((0, following, high_plane), (1, here, low_plane), (2, here, high_plane)):
        product = lax.dot_general(source, plane, last, preferred_element_type=f32)
        for tap in range(9):
            at = (k_z * 9 + tap) * 16
            weight_grads[at : at + 16, :] = product[:, tap * 128 : tap * 128 + 128].astype(bf16)
    turned = jnp.transpose(grads[...]).astype(bf16)
    for k_z in range(3):
        product = jnp.dot(
            own_unfolded[:, k_z * FINE : k_z * FINE + SLAB], turned, preferred_element_type=f32
        )
        weight_grads[432 + k_z * 144 : 576 + k_z * 144, :] = product.astype(bf16)
    rest = jnp.concatenate([second_grad[...], jnp.zeros((GRAD_ROWS - 1080, 128), f32)], axis=0)
    weight_grads[864:, :] = rest.astype(bf16)


def grad_sum_kernel(parts, spread):
    total = jnp.sum(parts[...].astype(f32), axis=0) * (1.0 / math.sqrt(SLAB))
    spread[...] = jnp.broadcast_to(total.astype(bf16)[None], spread.shape)


def grad_split_kernel(gathered, up, first_up, first_skip, second):
    values = gathered[...].reshape(GRAD_ROWS, 128).astype(f32)
    up[...] = values[:432].reshape(27, 16, 128)
    first = values[432:864].reshape(27, 16, 128)
    first_up[...] = first[:, :8]
    first_skip[...] = first[:, 8:]
    second[...] = values[864:1080].reshape(27, 8, 128)


def local(coarse, encoder_skip, up_weight, first_up, first_skip, second_weight, cotangent):
    slabs, shares = lax.axis_size("gz"), lax.axis_size("ch")
    upward = [(i, i + 1) for i in range(slabs - 1)]
    downward = [(i + 1, i) for i in range(slabs - 1)]

    def from_below(block):
        return lax.ppermute(block, "gz", upward)

    def from_above(block):
        return lax.ppermute(block, "gz", downward)

    def swap(block, axis):
        return lax.all_to_all(block, axis, 0, 0, tiled=True)

    def io_major(weight):
        return jnp.transpose(weight, (0, 2, 1))

    up_own, up_first = io_major(up_weight), io_major(first_up)
    skip_first, second_own = io_major(first_skip), io_major(second_weight)

    here = coarse.reshape(16, COARSE)
    halo = ((8, 2 * COARSE + 3 * FINE), bf16)
    upper, lower, own_skip, own_cot = call(
        halo_kernel,
        [halo, halo, ((8, SLAB), bf16), ((8, SLAB), bf16)],
        (here, encoder_skip, cotangent),
        [
            pltpu.VMEM((16, COARSE), bf16), pltpu.VMEM((8, 2, FINE), bf16), pltpu.VMEM((8, 2, FINE), bf16),
            pltpu.SemaphoreType.DMA((3,)),
        ],
        far=(0, 1, 2),
    )
    low, high = from_below(upper), from_above(lower)
    pieces = jnp.transpose(up_weight.reshape(27, 16, 8, 16), (1, 3, 0, 2)).reshape(16, 16, 216)
    mixed, pair, cot_planes = call(
        mix_kernel,
        [((16, 16, 640), bf16), ((2, 16, COARSE), bf16), ((32, SLAB), bf16)],
        (pieces, here, low, high, own_cot),
    )
    mixed, second_own, up_shared = lax.optimization_barrier((mixed, second_own, up_first))
    kernels = lax.all_gather(jnp.concatenate([second_own, up_shared], axis=1), "ch", axis=0)
    cot_planes = lax.all_gather(cot_planes, "ch", axis=0)

    partial, joined = call(
        up_kernel,
        [((16, 16, FINE + 128), bf16), ((16, HALOED), bf16)],
        (swap(mixed, "ch"), own_skip, low, high, up_first, skip_first),
        [pltpu.VMEM((144, HALOED), bf16)],
        near_outs=(1,),
    )
    pre, stats = call(
        first_sum_kernel,
        [((8, SLAB), f32), ((slabs, 16, FINE // 2 + 128), bf16)],
        (swap(partial, "ch"),),
    )
    (packed,) = call(
        first_norm_kernel, [((16, 16, SLAB + 128), bf16)], (pre, swap(stats, "gz"))
    )
    packed, kernels = lax.optimization_barrier((packed, kernels))
    packed = swap(packed, "ch")
    kept = [
        ((128, 3456), bf16), ((144, 3456), bf16), ((16, 3456), bf16), ((FINE, FINE), bf16), ((144, HALOED), bf16),
    ]
    forward, backward, first, up_matrix, interleave, first_unfolded = call(
        matrix_kernel,
        [((128, 3456), bf16)] + kept,
        (kernels, skip_first, up_own, joined),
        [pltpu.VMEM(*shape) for shape in kept] + [pltpu.SemaphoreType.DMA((5,))],
        10,
        far_outs=(1, 2, 3, 4, 5),
        near_outs=(0,),
    )
    unfolded = pltpu.VMEM((9, 128, HALOED), bf16)
    second_pre, halo, stats = call(
        second_conv_kernel,
        [
            ((128, SLAB), f32), ((128, SLAB), bf16), ((slabs, 2, 128), f32),
        ],
        (packed, forward),
        [unfolded],
        14,
        near=(1,),
        near_outs=(0, 1),
    )
    decoded, normed, slope, inverse, sums = call(
        second_norm_kernel,
        [
            ((8, SLAB), bf16), ((128, WIDE), f32), ((128, WIDE), f32), ((8, 128), f32),
            ((slabs, 2, 128), f32),
        ],
        (second_pre, from_below(halo), from_above(halo), swap(stats, "gz"), cot_planes),
        [pltpu.VMEM((16, 32, SLAB), bf16), pltpu.SemaphoreType.DMA((1,))],
        far=(4,),
        near=(0,),
        near_outs=(1, 2),
    )
    slope_one, sums, second_grad = call(
        second_back_kernel,
        [
            ((128, HALOED), f32), ((slabs, 2, 128), f32), ((216, 128), f32),
        ],
        (
            normed, slope, inverse, swap(sums, "gz"), packed, backward,
        ),
        [
            pltpu.VMEM((9, 128, WIDE), bf16), pltpu.VMEM((128, SLAB), f32), pltpu.VMEM((3, 128, 128), f32),
            pltpu.VMEM((128, 3456), bf16), pltpu.VMEM((144, HALOED), bf16), pltpu.SemaphoreType.DMA((1,)),
        ],
        20,
        far=(5,),
        near=(0, 1),
        near_outs=(0, 2),
    )
    skip_grad, coarse_own, coarse_next, weight_grads = call(
        first_back_kernel,
        [((8, SLAB), bf16), ((16, COARSE), f32), ((16, COARSE), f32), ((GRAD_ROWS, 128), bf16)],
        (
            slope_one, swap(sums, "gz"), packed, first,
            up_matrix, pair, first_unfolded, second_grad, interleave,
        ),
        [
            unfolded, pltpu.VMEM((128, SLAB), f32), pltpu.VMEM((3, 128, 128), f32),
            pltpu.VMEM((1152, 2 * COARSE), bf16), pltpu.VMEM((16, 3456), bf16),
            pltpu.VMEM((144, 3456), bf16), pltpu.VMEM((144, HALOED), bf16), pltpu.VMEM((FINE, FINE), bf16),
            pltpu.SemaphoreType.DMA((4,)),
        ],
        18,
        far=(3, 4, 6, 8),
        near=(0, 7),
    )
    coarse_grad = (coarse_own + from_below(coarse_next)).astype(bf16)
    rows = GRAD_ROWS // slabs
    (spread,) = call(
        grad_sum_kernel,
        [((slabs, rows, 128), bf16)],
        (swap(weight_grads.reshape(slabs, rows, 128), "gz"),),
    )
    grads = call(
        grad_split_kernel,
        [((27, 16, 128), f32), ((27, 8, 128), f32), ((27, 8, 128), f32), ((27, 8, 128), f32)],
        (swap(spread, "gz"),),
    )
    grads = [jnp.transpose(grad, (0, 2, 1)) for grad in grads]
    return (
        decoded.reshape(8, 2, FINE),
        coarse_grad.reshape(16, 1, COARSE),
        skip_grad.reshape(8, 2, FINE),
        *grads,
    )


def solution(mesh):
    volume, kernel = P("ch", "gz", None), P(None, None, "ch")
    return jax.shard_map(
        local,
        mesh=mesh,
        in_specs=(volume, volume, kernel, kernel, kernel, kernel, volume),
        out_specs=(volume, volume, volume, kernel, kernel, kernel, kernel),
        check_vma=False,
    )
```
